32 devices in a mesh: parts: 2 (over y), seq: 8 (over z, x), head: 2 (over core).
Axes of the slice: x: 2, y: 2, z: 4, core: 2. Of those that a mesh axis runs over, the one named last changes fastest.
Arguments:
- frames: bfloat16 [4096, 1024], P(('parts', 'seq'), 'head'), parts along dimension 0, may hold values from -40 to 40
- w_query: bfloat16 [1024, 1024], P(None, 'head'), may hold values from -0.1875 to 0.1875
- w_key: bfloat16 [1024, 1024], P(None, 'head'), may hold values from -0.1875 to 0.1875
- w_value: bfloat16 [1024, 1024], P(None, 'head'), may hold values from -0.1875 to 0.1875
- down_bank: bfloat16 [8, 1024, 128], P(None, 'seq'), may hold values from -0.1875 to 0.1875
- up_bank: bfloat16 [8, 128, 1024], P(None, 'seq', 'head'), may hold values from -0.75 to 0.75
- bank_row: int32 [8], replicated, may hold values from 0 to 7, each once
- lang_ids: int32 [16], P('parts'), parts along dimension 0, may hold values from 0 to 7, as said below
- seg_ids: int32 [16], P('parts'), parts along dimension 0, may hold values from 0 to 1, as said below
- lookback: int32 [16], P('parts'), parts along dimension 0, may hold values from 0 to 3, as said below
Outputs:
- context: bfloat16 [4096, 1024], P(('parts', 'seq'), 'head'), parts along dimension 0
The draws below stay inside these ranges and needn't reach their ends.
There are 2 independent parts, one for each index of `parts`. The reference program is written for one: setup_inputs(seed, part) draws one part's arguments, and reference() takes and returns one part's arrays. A program takes and returns all parts, laid end to end along the dimension named above; an argument that names none is the same for every part. Nothing has to cross between parts.
Inputs may be any that keep to these rules, and one draw needn't show every extreme that they name: `seg_ids`: blocks of one utterance are consecutive: the number is 0 at the first block and never falls; the largest number is reached at the last block. `lang_ids`: all blocks of one utterance have the same language; the last utterance has language 8 - 1. `bank_row`: each language names a different bank row. `lookback`: the value 3 is reached in every draw.
All inputs are finite; a program needn't handle non-finite values.
Results may differ from the reference program's by a relative error of at most 0.0093.
Values may be sent and summed in bfloat16 or wider, within the bound.
No kernel may reach another device: no remote copies, remote signals or barrier semaphores. Data moves between devices by JAX's collectives and lax.ppermute only.
A program may use at most 64 MiB of HBM per device.

```python
import math
import jax
import jax.numpy as jnp
from jax import lax

D = 1024
H = 16
HD = 64
R = 64
BLK = 256
FR_DEV = 256
FRAMES = 2048
BPD = 1
NBLK = 8
LOOK = 3
LANG = 8
N_SEQ = 8


def draw_frames(key, part):
    gaussian = jnp.clip(jax.random.normal(jax.random.fold_in(key, 1), (FRAMES, D), jnp.float32), -4.0, 4.0)
    return gaussian.astype(jnp.bfloat16)


def weight_pair(key):
    shared_normal = jnp.clip(jax.random.normal(jax.random.fold_in(key, 21), (D, D), jnp.float32), -6.0, 6.0)
    own_normal = jnp.clip(jax.random.normal(jax.random.fold_in(key, 22), (D, D), jnp.float32), -6.0, 6.0)
    return (shared_normal, own_normal)


def draw_w_query(key, part):
    shared_normal, own_normal = weight_pair(key)
    return (shared_normal / math.sqrt(D)).astype(jnp.bfloat16)


def draw_w_key(key, part):
    shared_normal, own_normal = weight_pair(key)
    return (own_normal / math.sqrt(D)).astype(jnp.bfloat16)


def block_tables(key):
    utterances = NBLK // (4 * BPD)
    shuffled = jax.random.permutation(jax.random.fold_in(key, 31), NBLK - 1) + 1
    cuts = shuffled[:utterances - 1]
    openings = jnp.zeros((NBLK,), jnp.int32).at[0].set(1).at[cuts].set(1)
    segments = jnp.cumsum(openings) - 1
    popular = jax.random.randint(jax.random.fold_in(key, 32), (4,), 0, LANG)
    which_popular = jax.random.randint(jax.random.fold_in(key, 33), (NBLK,), 0, 4)
    any_language = jax.random.randint(jax.random.fold_in(key, 34), (NBLK,), 0, LANG)
    favour = jax.random.randint(jax.random.fold_in(key, 35), (NBLK,), 0, 2) == 0
    seg_language = jnp.where(favour, popular[which_popular], any_language)
    last_segment = segments[NBLK - 1]
    seg_language = jnp.where(jnp.arange(NBLK, dtype=jnp.int32) == last_segment, LANG - 1, seg_language)
    return (segments.astype(jnp.int32), seg_language[segments].astype(jnp.int32))


def draw_seg_ids(key, part):
    segments, languages = block_tables(key)
    return segments


def draw_lang_ids(key, part):
    segments, languages = block_tables(key)
    return languages


def draw_lookback(key, part):
    longest = jax.random.randint(jax.random.fold_in(key, 41), (NBLK,), 0, 4) == 0
    spread = jax.random.randint(jax.random.fold_in(key, 42), (NBLK,), 0, LOOK + 1)
    reach_draw = jnp.where(longest, LOOK, spread)
    return reach_draw.at[NBLK - 1].set(LOOK).astype(jnp.int32)


def shard_levels(own_key, extent, pieces, low, top_value):
    def one(dim, parts):
        heights = jax.random.uniform(jax.random.fold_in(jax.random.fold_in(own_key, 6), dim), (parts,), jnp.float32, low / len(pieces), top_value / len(pieces))
        return jnp.repeat(jnp.exp(heights), extent[dim] // parts).reshape((-1,) + (1,) * (len(extent) - dim - 1))

    loudness = one(*pieces[0])
    for cut in pieces[1:]:
        loudness = loudness * one(*cut)
    return loudness


def bell_draw(stream_key, extent, deviation, limit, cuts=(), kind=jnp.bfloat16):
    result = jax.random.normal(stream_key, extent, jnp.float32) * deviation
    if len(cuts) > 0:
        result = shard_levels(stream_key, extent, cuts, -0.22, 0.18) * result
    return jnp.clip(result, min=-limit, max=limit).astype(kind)


def setup_inputs(seed: int = 0, part: int = 0) -> dict:
    keys = jax.random.split(jax.random.key(seed), 11)
    part_splits = jax.random.split(jax.random.fold_in(keys[10], part), 11)
    return {
        "frames": draw_frames(jax.random.fold_in(jax.random.fold_in(keys[10], part), 71), part),
        "w_query": draw_w_query(jax.random.fold_in(keys[10], 71), part),
        "w_key": draw_w_key(jax.random.fold_in(keys[10], 71), part),
        "w_value": bell_draw(keys[3], (D, D), D ** -0.5, 0.1875, ((1, 2),)),
        "down_bank": bell_draw(keys[4], (LANG, D, 2 * R), D ** -0.5, 0.1875, ((1, 8),)),
        "up_bank": bell_draw(keys[5], (LANG, 2 * R, D), R ** -0.5, 0.75, ((1, 8), (2, 2))),
        "bank_row": jax.random.permutation(keys[6], LANG).astype(jnp.int32),
        "lang_ids": draw_lang_ids(jax.random.fold_in(jax.random.fold_in(keys[10], part), 71), part),
        "seg_ids": draw_seg_ids(jax.random.fold_in(jax.random.fold_in(keys[10], part), 71), part),
        "lookback": draw_lookback(jax.random.fold_in(jax.random.fold_in(keys[10], part), 71), part),
    }


NEG_LARGE = -1.0e30


def reference(frames, w_query, w_key, w_value, down_bank, up_bank, bank_row, lang_ids, seg_ids, lookback):
    queries = jnp.dot(frames, w_query, preferred_element_type=jnp.float32).astype(jnp.bfloat16)
    queries = lax.optimization_barrier(queries)
    rows_used = jnp.take(bank_row, lang_ids, axis=0).astype(jnp.int32)
    block_rows = frames.reshape(NBLK, BLK, D).astype(jnp.float32)
    down_used = jnp.take(down_bank, rows_used, axis=0).astype(jnp.float32)
    lowrank = jnp.einsum("bfd,bdr->bfr", block_rows, down_used).astype(jnp.bfloat16)
    lowrank = lax.optimization_barrier(lowrank).astype(jnp.float32)
    up_used = jnp.take(up_bank, rows_used, axis=0).astype(jnp.float32)
    key_extra = jnp.einsum("bfr,brc->bfc", lowrank[:, :, :R], up_used[:, :R]).reshape(FRAMES, D)
    value_extra = jnp.einsum("bfr,brc->bfc", lowrank[:, :, R:], up_used[:, R:]).reshape(FRAMES, D)
    own_keys = (jnp.dot(frames, w_key, preferred_element_type=jnp.float32) + key_extra).astype(jnp.bfloat16)
    own_values = (jnp.dot(frames, w_value, preferred_element_type=jnp.float32) + value_extra).astype(jnp.bfloat16)
    own_keys = lax.optimization_barrier(own_keys)
    own_values = lax.optimization_barrier(own_values)
    pad_keys = jnp.concatenate([jnp.zeros((3 * FR_DEV, D), own_keys.dtype), own_keys], axis=0)
    pad_values = jnp.concatenate([jnp.zeros((3 * FR_DEV, D), own_values.dtype), own_values], axis=0)
    pad_seg = jnp.concatenate([jnp.full((3 * BPD,), -1, jnp.int32), seg_ids.astype(jnp.int32)])

    def one_shard(shard_index):
        query_first = (shard_index * BPD).astype(jnp.int32)
        query_blocks = query_first + jnp.arange(BPD, dtype=jnp.int32)
        key_blocks = query_first - 3 * BPD + jnp.arange(4 * BPD, dtype=jnp.int32)
        query_seg = lax.dynamic_slice_in_dim(seg_ids.astype(jnp.int32), query_first, BPD)
        query_reach = lax.dynamic_slice_in_dim(lookback.astype(jnp.int32), query_first, BPD)
        key_seg = lax.dynamic_slice_in_dim(pad_seg, query_first, 4 * BPD)
        allowed = key_blocks[None, :] >= query_blocks[:, None] - query_reach[:, None]
        allowed = allowed & (key_blocks[None, :] <= query_blocks[:, None])
        allowed = allowed & (key_seg[None, :] == query_seg[:, None]) & (key_blocks[None, :] >= 0)
        frame_mask = jnp.broadcast_to(allowed[:, None, :, None], (BPD, BLK, 4 * BPD, BLK)).reshape(FR_DEV, 4 * FR_DEV)
        frame_first = (shard_index * FR_DEV).astype(jnp.int32)
        query_part = lax.dynamic_slice_in_dim(queries, frame_first, FR_DEV).reshape(FR_DEV, H, HD).astype(jnp.float32)
        key_part = lax.dynamic_slice_in_dim(pad_keys, frame_first, 4 * FR_DEV).reshape(4 * FR_DEV, H, HD).astype(jnp.float32)
        value_part = lax.dynamic_slice_in_dim(pad_values, frame_first, 4 * FR_DEV).reshape(4 * FR_DEV, H, HD).astype(jnp.float32)
        scores = jnp.einsum("qhe,khe->hqk", query_part, key_part) * (HD ** -0.5)
        masked = jnp.where(frame_mask[None], scores, NEG_LARGE)
        row_max = jnp.max(masked, axis=2, keepdims=True)
        weights = jnp.where(frame_mask[None], jnp.exp(masked - row_max), 0.0)
        row_total = jnp.sum(weights, axis=2)
        rounded = lax.optimization_barrier(weights.astype(jnp.bfloat16)).astype(jnp.float32)
        context = jnp.einsum("hqk,khe->qhe", rounded, value_part) / jnp.transpose(row_total)[:, :, None]
        return context.reshape(FR_DEV, D).astype(jnp.bfloat16)

    shards = lax.map(one_shard, jnp.arange(N_SEQ, dtype=jnp.int32))
    return shards.reshape(FRAMES, D)
```

```python
import functools

import jax
import jax.numpy as jnp
from jax import lax
from jax.experimental import pallas as pl
from jax.experimental.pallas import tpu as pltpu
from jax.sharding import PartitionSpec as P

HD = 64
LANES = 128
LOOK = 3
NEG_LARGE = -1e30
F32 = jnp.float32
BF16 = jnp.bfloat16

VMEM = functools.partial(pl.BlockSpec, memory_space=pltpu.VMEM)
SMEM = functools.partial(pl.BlockSpec, memory_space=pltpu.SMEM)
ANY = functools.partial(pl.BlockSpec, memory_space=pl.ANY)


def mm(a, b):
    return jnp.dot(a, b, preferred_element_type=F32)


def reach(seg_ref, look_ref, position):
    count = jnp.int32(0)
    for distance in range(1, LOOK + 1):
        earlier = jnp.maximum(position - distance, 0)
        allowed = (
            (position >= distance)
            & (look_ref[position] >= distance)
            & (seg_ref[earlier] == seg_ref[position])
        )
        count = count + allowed.astype(jnp.int32)
    return count


def pack_kernel(row_ref, lang_ref, down_ref, up_ref, out_ref, sems):
    head = lax.axis_index("head")
    count = out_ref.shape[0]
    half = down_ref.shape[1] // 2
    depth = up_ref.shape[1]
    chunks = up_ref.shape[2] // LANES

    def copies(j):
        row = row_ref[lang_ref[j]]
        yield pltpu.make_async_copy(
            down_ref.at[row, pl.ds(pl.multiple_of(head * half, half), half), :],
            out_ref.at[j, pl.ds(0, half), :],
            sems.at[j, 0],
        )
        for c in range(chunks):
            yield pltpu.make_async_copy(
                up_ref.at[row, :, pl.ds(c * LANES, LANES)],
                out_ref.at[j, pl.ds(half + c * depth, depth), :],
                sems.at[j, c + 1],
            )

    @pl.loop(0, count)
    def _(j):
        for copy in copies(j):
            copy.start()

    @pl.loop(0, count)
    def _(j):
        for copy in copies(j):
            copy.wait()


def pack(bank_row, lang_ids, down_bank, up_bank, count):
    rows = down_bank.shape[1] // 2 + up_bank.shape[1] * (up_bank.shape[2] // LANES)
    return pl.pallas_call(
        pack_kernel,
        out_shape=jax.ShapeDtypeStruct((count, rows, LANES), BF16),
        in_specs=[SMEM(), SMEM(), ANY(), ANY()],
        out_specs=ANY(),
        scratch_shapes=[pltpu.SemaphoreType.DMA((count, 1 + up_bank.shape[2] // LANES))],
    )(bank_row, lang_ids, down_bank, up_bank)


def keys_values(first, second, head, wk_ref, wv_ref, down_ref, up_ref):
    half = first.shape[1]
    mine = pl.ds(pl.multiple_of(head * half, half), half)
    other = pl.ds(pl.multiple_of((1 - head) * half, half), half)
    lowrank = mm(first, down_ref[mine, :]) + mm(second, down_ref[other, :])
    lowrank = lowrank.astype(BF16)
    lane = lax.broadcasted_iota(jnp.int32, lowrank.shape, 1)
    split = lowrank.shape[1] // 2
    zero = jnp.zeros_like(lowrank)
    low_key = jnp.where(lane < split, lowrank, zero)
    low_value = jnp.where(lane < split, zero, lowrank)
    up = up_ref[...]
    keys = mm(first, wk_ref[mine, :]) + mm(second, wk_ref[other, :]) + mm(low_key, up)
    values = mm(first, wv_ref[mine, :]) + mm(second, wv_ref[other, :]) + mm(low_value, up)
    return keys.astype(BF16), values.astype(BF16)


def attend(q_ref, keys, values, acc_ref, max_ref, opening):
    rows = q_ref.shape[0]
    heads = acc_ref.shape[0]
    lane = lax.broadcasted_iota(jnp.int32, (rows, LANES), 1)
    for i in range(heads):
        cols = slice(i // 2 * LANES, (i // 2 + 1) * LANES)
        inside = (lane < HD) if i % 2 == 0 else (lane >= HD)
        q = q_ref[:, cols]
        q = jnp.where(inside, q, jnp.zeros_like(q))
        scores = lax.dot_general(
            q, keys[:, cols], (((1,), (1,)), ((), ())), preferred_element_type=F32
        )
        v = values[:, cols]
        v = jnp.where(inside[: v.shape[0]], v, jnp.ones_like(v))
        top = jnp.max(scores, axis=1, keepdims=True)
        if not opening:
            before = max_ref[i][:, :1]
            top = jnp.maximum(top, before)
        weights = jnp.exp(scores - top).astype(BF16)
        update = mm(weights, v)
        if not opening:
            update = acc_ref[i] * jnp.exp(before - top) + update
        acc_ref[i] = update
        max_ref[i] = jnp.broadcast_to(top, (rows, LANES))


def finish(acc_ref, out_ref):
    rows = out_ref.shape[0]
    heads = acc_ref.shape[0]
    lane = lax.broadcasted_iota(jnp.int32, (rows, LANES), 1)
    for pair in range(heads // 2):
        even = acc_ref[2 * pair]
        odd = acc_ref[2 * pair + 1]
        total = jnp.where(lane < HD, odd, even)
        total = pltpu.roll(total, HD, 1)
        value = jnp.where(lane < HD, even, odd)
        out_ref[:, pair * LANES : (pair + 1) * LANES] = (value / total).astype(BF16)


def early_kernel(
    packed, seg_ref, look_ref, a0, b0, a1, b1, a2, b2, got, other, wq, wk, wv,
    q_ref, acc_ref, max_ref, down_ref, up_ref,
):
    head = lax.axis_index("head")
    position = lax.axis_index("seq")
    count = reach(seg_ref, look_ref, position)
    if packed:
        half = other.shape[1]
        depth = up_ref.shape[0] // got.shape[0]
        for j in range(got.shape[0]):
            base = j * 2 * half
            down_ref[pl.ds(pl.multiple_of(base + head * half, half), half), :] = got[j, :half, :]
            down_ref[pl.ds(pl.multiple_of(base + (1 - head) * half, half), half), :] = other[j]
        for c in range(up_ref.shape[1] // LANES):
            piece = got[:, half + c * depth : half + (c + 1) * depth, :]
            up_ref[:, c * LANES : (c + 1) * LANES] = piece.reshape(up_ref.shape[0], LANES)
    else:
        down_ref[...] = got[...]
        up_ref[...] = other[...]
    width = a0.shape[1]
    mine = pl.ds(pl.multiple_of(head * width, width), width)
    others = pl.ds(pl.multiple_of((1 - head) * width, width), width)
    queries = (mm(a0[...], wq[mine, :]) + mm(b0[...], wq[others, :])).astype(BF16)
    q_ref[...] = queries * jnp.asarray(HD**-0.5, BF16)
    for distance, (a, b) in enumerate(((a0, b0), (a1, b1), (a2, b2))):

        def visit(a=a, b=b, opening=distance == 0):
            keys, values = keys_values(a[...], b[...], head, wk, wv, down_ref, up_ref)
            attend(q_ref, keys, values, acc_ref, max_ref, opening)

        if distance:
            pl.when(count >= distance)(visit)
        else:
            visit()


def late_kernel(
    seg_ref, look_ref, a3, b3, q_ref, acc_in, max_in, down_ref, up_ref, wk, wv,
    out_ref, acc_ref, max_ref,
):
    head = lax.axis_index("head")
    position = lax.axis_index("seq")
    count = reach(seg_ref, look_ref, position)

    @pl.when(count >= LOOK)
    def _():
        acc_ref[...] = acc_in[...]
        max_ref[...] = max_in[...]
        keys, values = keys_values(a3[...], b3[...], head, wk, wv, down_ref, up_ref)
        attend(q_ref, keys, values, acc_ref, max_ref, False)
        finish(acc_ref, out_ref)

    @pl.when(count < LOOK)
    def _():
        finish(acc_in, out_ref)


def body(
    frames, w_query, w_key, w_value, down_bank, up_bank, bank_row, lang_ids, seg_ids, lookback
):
    count = lax.axis_size("seq")
    rows, width = frames.shape
    columns = w_query.shape[1]
    heads = columns // HD
    model_width = w_query.shape[0]
    rank_two = down_bank.shape[2]

    def shift(x, distance):
        return lax.ppermute(x, "seq", [(i, (i + distance) % count) for i in range(count)])

    def swap(x):
        return lax.ppermute(x, "head", [(0, 1), (1, 0)])

    a0 = frames
    a2 = shift(a0, 2)
    a1 = shift(a0, 1)
    a3 = shift(a2, 1)
    b0, b1, b2, b3 = swap(a0), swap(a1), swap(a2), swap(a3)

    packed = down_bank.shape[1] % 32 == 0 and up_bank.shape[1] % 16 == 0
    if packed:
        sent = pack(bank_row, lang_ids, down_bank, up_bank, count)
        got = lax.all_to_all(sent, "seq", split_axis=0, concat_axis=0, tiled=True)
        other = swap(got[:, : down_bank.shape[1] // 2, :])
    else:
        wanted = jnp.take(bank_row, lang_ids, axis=0)
        got = lax.all_to_all(
            jnp.take(down_bank, wanted, axis=0), "seq", split_axis=0, concat_axis=0, tiled=True
        ).reshape(model_width, rank_two)
        other = lax.all_to_all(
            jnp.take(up_bank, wanted, axis=0), "seq", split_axis=0, concat_axis=0, tiled=True
        ).reshape(rank_two, columns)

    state = jax.ShapeDtypeStruct((heads, rows, LANES), F32)
    q, acc, top, down, up = pl.pallas_call(
        functools.partial(early_kernel, packed),
        out_shape=(
            jax.ShapeDtypeStruct((rows, columns), BF16),
            state,
            state,
            jax.ShapeDtypeStruct((model_width, rank_two), BF16),
            jax.ShapeDtypeStruct((rank_two, columns), BF16),
        ),
        in_specs=[SMEM(), SMEM()] + [VMEM()] * 11,
        out_specs=(VMEM(),) * 5,
        compiler_params=pltpu.CompilerParams(vmem_limit_bytes=32 * 1024 * 1024),
    )(seg_ids, lookback, a0, b0, a1, b1, a2, b2, got, other, w_query, w_key, w_value)
    return pl.pallas_call(
        late_kernel,
        out_shape=jax.ShapeDtypeStruct((rows, columns), BF16),
        in_specs=[SMEM(), SMEM()] + [VMEM()] * 9,
        out_specs=VMEM(),
        scratch_shapes=[pltpu.VMEM(state.shape, F32)] * 2,
        compiler_params=pltpu.CompilerParams(vmem_limit_bytes=32 * 1024 * 1024),
    )(seg_ids, lookback, a3, b3, q, acc, top, down, up, w_key, w_value)


def solution(mesh):
    in_specs = (
        P(("parts", "seq"), "head"),
        P(None, "head"),
        P(None, "head"),
        P(None, "head"),
        P(None, "seq", None),
        P(None, "seq", "head"),
        P(),
        P("parts"),
        P("parts"),
        P("parts"),
    )
    out_specs = P(("parts", "seq"), "head")
    return jax.shard_map(body, mesh=mesh, in_specs=in_specs, out_specs=out_specs, check_vma=False)
```

```python
import functools

import jax
import jax.numpy as jnp
from jax import lax
from jax.experimental import pallas as pl
from jax.experimental.pallas import tpu as pltpu
from jax.sharding import PartitionSpec as P

HD = 64
LANES = 128
LOOK = 3
VMEM_BYTES = 8 * 1024 * 1024
F32 = jnp.float32
BF16 = jnp.bfloat16

VMEM = functools.partial(pl.BlockSpec, memory_space=pltpu.VMEM)
SMEM = functools.partial(pl.BlockSpec, memory_space=pltpu.SMEM)


def mm(a, b):
    return jnp.dot(a, b, preferred_element_type=F32)


def reach(seg_ref, look_ref, position):
    count = jnp.int32(0)
    for distance in range(1, LOOK + 1):
        earlier = jnp.maximum(position - distance, 0)
        allowed = (
            (position >= distance)
            & (look_ref[position] >= distance)
            & (seg_ref[earlier] == seg_ref[position])
        )
        count = count + allowed.astype(jnp.int32)
    return count


def pack_kernel(row_ref, lang_ref, down_ref, up_ref, out_ref):
    head = lax.axis_index("head")
    half = down_ref.shape[1] // 2
    depth = up_ref.shape[1]
    mine = pl.ds(pl.multiple_of(head * half, half), half)
    for j in range(out_ref.shape[0]):
        row = row_ref[lang_ref[j]]
        out_ref[j, :half, :] = down_ref[row, mine, :]
        for c in range(up_ref.shape[2] // LANES):
            out_ref[j, half + c * depth : half + (c + 1) * depth, :] = up_ref[
                row, :, c * LANES : (c + 1) * LANES
            ]


def pack(bank_row, lang_ids, down_bank, up_bank, count):
    rows = down_bank.shape[1] // 2 + up_bank.shape[1] * (up_bank.shape[2] // LANES)
    return pl.pallas_call(
        pack_kernel,
        out_shape=jax.ShapeDtypeStruct((count, rows, LANES), BF16),
        in_specs=[SMEM(), SMEM(), VMEM(), VMEM()],
        out_specs=VMEM(),
        compiler_params=pltpu.CompilerParams(vmem_limit_bytes=VMEM_BYTES),
    )(bank_row, lang_ids, down_bank, up_bank)


def halves(head, width):
    mine = pl.ds(pl.multiple_of(head * width, width), width)
    other = pl.ds(pl.multiple_of((1 - head) * width, width), width)
    return mine, other


def query_kernel(a, b, wq, q_ref):
    mine, other = halves(lax.axis_index("head"), a.shape[1])
    queries = (mm(a[...], wq[mine, :]) + mm(b[...], wq[other, :])).astype(BF16)
    q_ref[...] = (queries * jnp.asarray(HD**-0.5, BF16)).T


def unpack(got, other, down_ref, up_ref):
    head = lax.axis_index("head")
    half = other.shape[1]
    depth = up_ref.shape[0] // got.shape[0]
    for j in range(got.shape[0]):
        for part, source in ((head, got), (1 - head, other)):
            place = pl.ds(pl.multiple_of(j * 2 * half + part * half, half), half)
            down_ref[place, :] = source[j, :half, :]
    for c in range(up_ref.shape[1] // LANES):
        piece = got[:, half + c * depth : half + (c + 1) * depth, :]
        up_ref[:, c * LANES : (c + 1) * LANES] = piece.reshape(up_ref.shape[0], LANES)


def keys_values(a, b, wk, wv, down_ref, up_ref):
    mine, other = halves(lax.axis_index("head"), a.shape[1])
    first, second = a[...], b[...]
    lowrank = mm(first, down_ref[mine, :]) + mm(second, down_ref[other, :])
    lowrank = lowrank.astype(BF16)
    lane = lax.broadcasted_iota(jnp.int32, lowrank.shape, 1)
    split = lowrank.shape[1] // 2
    zero = jnp.zeros_like(lowrank)
    low_key = jnp.where(lane < split, lowrank, zero)
    low_value = jnp.where(lane < split, zero, lowrank)
    up = up_ref[...]
    keys = mm(first, wk[mine, :]) + mm(second, wk[other, :]) + mm(low_key, up)
    values = mm(first, wv[mine, :]) + mm(second, wv[other, :]) + mm(low_value, up)
    return keys.astype(BF16), values.astype(BF16)


def attend(q_ref, keys, values, before, after):
    turned = values.T
    ones = jnp.ones((16, turned.shape[1]), BF16)
    acc_ref, max_ref = after
    for i in range(acc_ref.shape[0]):
        rows = slice(i * HD, (i + 1) * HD)
        q = q_ref[rows, :]
        zero = jnp.zeros_like(q)
        q = jnp.concatenate([q, zero] if i % 2 == 0 else [zero, q], axis=0)
        scores = mm(keys[:, i // 2 * LANES : (i // 2 + 1) * LANES], q)
        top = jnp.max(scores, axis=0, keepdims=True)
        if before is not None:
            old = before[1][i : i + 1, :]
            top = jnp.maximum(top, old)
        weights = jnp.exp(scores - top).astype(BF16)
        update = mm(jnp.concatenate([turned[rows, :], ones], axis=0), weights)
        update = update[: acc_ref.shape[1], :]
        if before is not None:
            update = before[0][i] * jnp.exp(old - top) + update
        acc_ref[i] = update
        max_ref[i : i + 1, :] = top


def finish(acc_ref, out_ref):
    for pair in range(acc_ref.shape[0] // 2):
        parts = []
        for i in (2 * pair, 2 * pair + 1):
            parts.append(acc_ref[i, :HD, :] / acc_ref[i, HD : HD + 1, :])
        out_ref[:, pair * LANES : (pair + 1) * LANES] = (
            jnp.concatenate(parts, axis=0).T.astype(BF16)
        )


def opening_kernel(packed, got, other, a, b, q_ref, wk, wv, acc_ref, max_ref, down_ref, up_ref):
    if packed:
        unpack(got, other, down_ref, up_ref)
    else:
        down_ref[...] = got[...]
        up_ref[...] = other[...]
    keys, values = keys_values(a, b, wk, wv, down_ref, up_ref)
    attend(q_ref, keys, values, None, (acc_ref, max_ref))


def block_kernel(
    distance, closing, seg_ref, look_ref, a, b, q_ref, wk, wv, down_ref, up_ref, acc_in, max_in, *outs
):
    count = reach(seg_ref, look_ref, lax.axis_index("seq"))
    if closing:
        out_ref, acc_ref, max_ref = outs
    else:
        acc_ref, max_ref = outs

    @pl.when(count >= distance)
    def _():
        keys, values = keys_values(a, b, wk, wv, down_ref, up_ref)
        attend(q_ref, keys, values, (acc_in, max_in), (acc_ref, max_ref))
        if closing:
            finish(acc_ref, out_ref)

    @pl.when(count < distance)
    def _():
        if closing:
            finish(acc_in, out_ref)
        else:
            acc_ref[...] = acc_in[...]
            max_ref[...] = max_in[...]


def body(
    frames, w_query, w_key, w_value, down_bank, up_bank, bank_row, lang_ids, seg_ids, lookback
):
    count = lax.axis_size("seq")
    rows, width = frames.shape
    columns = w_query.shape[1]
    heads = columns // HD
    model_width = w_query.shape[0]
    rank_two = down_bank.shape[2]
    params = pltpu.CompilerParams(vmem_limit_bytes=VMEM_BYTES)

    def shift(x, distance):
        return lax.ppermute(x, "seq", [(i, (i + distance) % count) for i in range(count)])

    def swap(x):
        return lax.ppermute(x, "head", [(0, 1), (1, 0)])

    a0 = frames
    a2 = shift(a0, 2)
    a1 = shift(a0, 1)
    a3 = shift(a2, 1)
    b0, b1, b2, b3 = swap(a0), swap(a1), swap(a2), swap(a3)

    packed = down_bank.shape[1] % 32 == 0 and up_bank.shape[1] % 16 == 0
    if packed:
        sent = pack(bank_row, lang_ids, down_bank, up_bank, count)
        got = lax.all_to_all(sent, "seq", split_axis=0, concat_axis=0, tiled=True)
        other = swap(got[:, : down_bank.shape[1] // 2, :])
    else:
        wanted = jnp.take(bank_row, lang_ids, axis=0)
        got = lax.all_to_all(
            jnp.take(down_bank, wanted, axis=0), "seq", split_axis=0, concat_axis=0, tiled=True
        ).reshape(model_width, rank_two)
        other = lax.all_to_all(
            jnp.take(up_bank, wanted, axis=0), "seq", split_axis=0, concat_axis=0, tiled=True
        ).reshape(rank_two, columns)

    q = pl.pallas_call(
        query_kernel,
        out_shape=jax.ShapeDtypeStruct((columns, rows), BF16),
        in_specs=[VMEM()] * 3,
        out_specs=VMEM(),
        compiler_params=params,
    )(a0, b0, w_query)
    state = (
        jax.ShapeDtypeStruct((heads, HD + 8, rows), F32),
        jax.ShapeDtypeStruct((heads, rows), F32),
    )
    acc, top, down, up = pl.pallas_call(
        functools.partial(opening_kernel, packed),
        out_shape=state
        + (
            jax.ShapeDtypeStruct((model_width, rank_two), BF16),
            jax.ShapeDtypeStruct((rank_two, columns), BF16),
        ),
        in_specs=[VMEM()] * 7,
        out_specs=(VMEM(),) * 4,
        compiler_params=params,
    )(got, other, a0, b0, q, w_key, w_value)
    for distance, a, b in ((2, a2, b2), (1, a1, b1), (3, a3, b3)):
        closing = distance == LOOK
        result = pl.pallas_call(
            functools.partial(block_kernel, distance, closing),
            out_shape=jax.ShapeDtypeStruct((rows, columns), BF16) if closing else state,
            in_specs=[SMEM(), SMEM()] + [VMEM()] * 9,
            out_specs=VMEM() if closing else (VMEM(), VMEM()),
            scratch_shapes=[pltpu.VMEM(s.shape, F32) for s in state] if closing else [],
            compiler_params=params,
        )(seg_ids, lookback, a, b, q, w_key, w_value, down, up, acc, top)
        if not closing:
            acc, top = result
    return result


def solution(mesh):
    in_specs = (
        P(("parts", "seq"), "head"),
        P(None, "head"),
        P(None, "head"),
        P(None, "head"),
        P(None, "seq", None),
        P(None, "seq", "head"),
        P(),
        P("parts"),
        P("parts"),
        P("parts"),
    )
    out_specs = P(("parts", "seq"), "head")
    return jax.shard_map(body, mesh=mesh, in_specs=in_specs, out_specs=out_specs, check_vma=False)
```

```python
import functools

import jax
import jax.numpy as jnp
from jax import lax
from jax.experimental import pallas as pl
from jax.experimental.pallas import tpu as pltpu
from jax.sharding import PartitionSpec as P

HD = 64
LANES = 128
LOOK = 3
VMEM_BYTES = 8 * 1024 * 1024
F32 = jnp.float32
BF16 = jnp.bfloat16

VMEM = functools.partial(pl.BlockSpec, memory_space=pltpu.VMEM)
HBM = functools.partial(pl.BlockSpec, memory_space=pltpu.HBM)


def mm(a, b):
    return jnp.dot(a, b, preferred_element_type=F32)


def reach(seg_ref, look_ref, position):
    count = jnp.int32(0)
    for distance in range(1, LOOK + 1):
        earlier = jnp.maximum(position - distance, 0)
        allowed = (
            (position >= distance)
            & (look_ref[position] >= distance)
            & (seg_ref[earlier] == seg_ref[position])
        )
        count = count + allowed.astype(jnp.int32)
    return count


def rules_kernel(
    packed, row_hbm, lang_hbm, seg_hbm, look_hbm, down_hbm, up_hbm, *refs
):
    if packed:
        reach_ref, out_ref, row, lang, seg, look, down, up, sems = refs
        pairs = [(row_hbm, row), (lang_hbm, lang), (seg_hbm, seg), (look_hbm, look)]
        pairs += [(down_hbm, down), (up_hbm, up)]
    else:
        reach_ref, seg, look, sems = refs
        pairs = [(seg_hbm, seg), (look_hbm, look)]
    copies = [pltpu.make_async_copy(a, b, sems.at[k]) for k, (a, b) in enumerate(pairs)]
    for copy in copies:
        copy.start()
    for copy in copies:
        copy.wait()
    count = reach(seg, look, lax.axis_index("seq"))
    reach_ref[...] = jnp.full(reach_ref.shape, count, jnp.int32)
    if packed:
        half = down.shape[1] // 2
        depth = up.shape[1]
        mine = pl.ds(pl.multiple_of(lax.axis_index("head") * half, half), half)
        for j in range(out_ref.shape[0]):
            chosen = row[lang[j]]
            out_ref[j, :half, :] = down[chosen, mine, :]
            for c in range(up.shape[2] // LANES):
                out_ref[j, half + c * depth : half + (c + 1) * depth, :] = up[
                    chosen, :, c * LANES : (c + 1) * LANES
                ]


def cost(microseconds):
    return pl.CostEstimate(flops=int(microseconds * 1e9), bytes_accessed=0, transcendentals=0)


def rules(packed, bank_row, lang_ids, seg_ids, lookback, down_bank, up_bank, count):
    rows = down_bank.shape[1] // 2 + up_bank.shape[1] * (up_bank.shape[2] // LANES)
    out_shape = [jax.ShapeDtypeStruct((8, LANES), jnp.int32)]
    tables = [seg_ids, lookback]
    scratch = []
    if packed:
        out_shape.append(jax.ShapeDtypeStruct((count, rows, LANES), BF16))
        tables = [bank_row, lang_ids] + tables
        scratch = [pltpu.VMEM(down_bank.shape, BF16), pltpu.VMEM(up_bank.shape, BF16)]
    scratch = [pltpu.SMEM(t.shape, jnp.int32) for t in tables] + scratch
    return pl.pallas_call(
        functools.partial(rules_kernel, packed),
        out_shape=out_shape,
        in_specs=[HBM()] * 6,
        out_specs=[VMEM()] * len(out_shape),
        scratch_shapes=scratch + [pltpu.SemaphoreType.DMA((len(scratch),))],
        compiler_params=pltpu.CompilerParams(vmem_limit_bytes=VMEM_BYTES),
        cost_estimate=cost(2),
    )(
        *(
            pltpu.with_memory_space_constraint(x, pltpu.HBM)
            for x in (bank_row, lang_ids, seg_ids, lookback, down_bank, up_bank)
        )
    )


def halves(head, width):
    mine = pl.ds(pl.multiple_of(head * width, width), width)
    other = pl.ds(pl.multiple_of((1 - head) * width, width), width)
    return mine, other


def query_kernel(a, b, wq, wk, wv, q_ref):
    mine, other = halves(lax.axis_index("head"), a.shape[1])
    queries = (mm(a[...], wq[mine, :]) + mm(b[...], wq[other, :])).astype(BF16)
    q_ref[...] = (queries * jnp.asarray(HD**-0.5, BF16)).T


def lower_kernel(got, b_ref, q_ref, half_ref):
    half_ref[...] = got[:, : half_ref.shape[1], :]


def unpack(got, other, down_ref, up_ref):
    head = lax.axis_index("head")
    half = other.shape[1]
    depth = up_ref.shape[0] // got.shape[0]
    for j in range(got.shape[0]):
        for part, source in ((head, got), (1 - head, other)):
            place = pl.ds(pl.multiple_of(j * 2 * half + part * half, half), half)
            down_ref[place, :] = source[j, :half, :]
    for c in range(up_ref.shape[1] // LANES):
        piece = got[:, half + c * depth : half + (c + 1) * depth, :]
        up_ref[:, c * LANES : (c + 1) * LANES] = piece.reshape(up_ref.shape[0], LANES)


def keys_values(a, b, wk, wv, down_ref, up_ref):
    mine, other = halves(lax.axis_index("head"), a.shape[1])
    first, second = a[...], b[...]
    lowrank = mm(first, down_ref[mine, :]) + mm(second, down_ref[other, :])
    lowrank = lowrank.astype(BF16)
    lane = lax.broadcasted_iota(jnp.int32, lowrank.shape, 1)
    split = lowrank.shape[1] // 2
    zero = jnp.zeros_like(lowrank)
    low_key = jnp.where(lane < split, lowrank, zero)
    low_value = jnp.where(lane < split, zero, lowrank)
    up = up_ref[...]
    keys = mm(first, wk[mine, :]) + mm(second, wk[other, :]) + mm(low_key, up)
    values = mm(first, wv[mine, :]) + mm(second, wv[other, :]) + mm(low_value, up)
    return keys.astype(BF16), values.astype(BF16)


def attend(q_ref, keys, values, before, after, weights_ref):
    turned = values.T
    ones = jnp.ones((16, turned.shape[1]), BF16)
    acc_ref, max_ref = after
    heads = acc_ref.shape[0]
    factors = []
    for i in range(heads):
        q = q_ref[i * HD : (i + 1) * HD, :]
        zero = jnp.zeros_like(q)
        q = jnp.concatenate([q, zero] if i % 2 == 0 else [zero, q], axis=0)
        scores = mm(keys[:, i // 2 * LANES : (i // 2 + 1) * LANES], q)
        top = jnp.max(scores, axis=0, keepdims=True)
        if before is not None:
            old = before[1][i : i + 1, :]
            top = jnp.maximum(top, old)
            factors.append(jnp.exp(old - top))
        weights_ref[i] = jnp.exp(scores - top).astype(BF16)
        max_ref[i : i + 1, :] = top
    for i in range(heads):
        left = jnp.concatenate([turned[i * HD : (i + 1) * HD, :], ones], axis=0)
        update = mm(left, weights_ref[i])[: acc_ref.shape[1], :]
        if before is not None:
            update = before[0][i] * factors[i] + update
        acc_ref[i] = update


def finish(acc_ref, out_ref):
    for pair in range(acc_ref.shape[0] // 2):
        parts = []
        for i in (2 * pair, 2 * pair + 1):
            parts.append(acc_ref[i, :HD, :] / acc_ref[i, HD : HD + 1, :])
        out_ref[:, pair * LANES : (pair + 1) * LANES] = (
            jnp.concatenate(parts, axis=0).T.astype(BF16)
        )


def opening_kernel(
    packed, got, other, reach_ref, a0, b0, a2_hbm, b2_hbm, a1_hbm, b1_hbm, q_ref, wk, wv,
    acc_ref, max_ref, down_ref, up_ref, token_ref, a2, b2, a1, b1, weights_ref, sems,
):
    pairs = ((a2_hbm, a2), (b2_hbm, b2), (a1_hbm, a1), (b1_hbm, b1))
    copies = [pltpu.make_async_copy(x, y, sems.at[k]) for k, (x, y) in enumerate(pairs)]
    for copy in copies:
        copy.start()
    token_ref[...] = reach_ref[...]
    if packed:
        unpack(got, other, down_ref, up_ref)
    else:
        down_ref[...] = got[...]
        up_ref[...] = other[...]
    state = (acc_ref, max_ref)
    keys, values = keys_values(a0, b0, wk, wv, down_ref, up_ref)
    attend(q_ref, keys, values, None, state, weights_ref)
    for copy in copies:
        copy.wait()
    count = reach_ref[0, 0]

    @pl.when(count >= 2)
    def _():
        keys, values = keys_values(a2, b2, wk, wv, down_ref, up_ref)
        attend(q_ref, keys, values, state, state, weights_ref)

    @pl.when((lax.axis_index("seq") % 2 == 1) & (count >= 1))
    def _():
        keys, values = keys_values(a1, b1, wk, wv, down_ref, up_ref)
        attend(q_ref, keys, values, state, state, weights_ref)


def block_kernel(
    distances, reach_ref, a, b, q_ref, wk, wv, down_ref, up_ref, acc_in, max_in,
    acc_ref, max_ref, weights_ref,
):
    odd = lax.axis_index("seq") % 2
    even_distance, odd_distance = distances
    distance = jnp.where(odd == 1, odd_distance, even_distance)

    @pl.when(reach_ref[0, 0] >= distance)
    def _():
        keys, values = keys_values(a, b, wk, wv, down_ref, up_ref)
        attend(q_ref, keys, values, (acc_in, max_in), (acc_ref, max_ref), weights_ref)


def closing_kernel(
    distances, reach_ref, a, b, q_ref, wk, wv, down_ref, up_ref, acc_in, max_in,
    out_ref, acc_ref, max_ref, weights_ref,
):
    odd = lax.axis_index("seq") % 2
    even_distance, odd_distance = distances
    distance = jnp.where(odd == 1, odd_distance, even_distance)
    needed = reach_ref[0, 0] >= distance

    @pl.when(needed)
    def _():
        keys, values = keys_values(a, b, wk, wv, down_ref, up_ref)
        attend(q_ref, keys, values, (acc_in, max_in), (acc_ref, max_ref), weights_ref)
        finish(acc_ref, out_ref)

    @pl.when(jnp.logical_not(needed))
    def _():
        finish(acc_in, out_ref)


def body(
    frames, w_query, w_key, w_value, down_bank, up_bank, bank_row, lang_ids, seg_ids, lookback
):
    count = lax.axis_size("seq")
    rows, width = frames.shape
    columns = w_query.shape[1]
    heads = columns // HD
    model_width = w_query.shape[0]
    rank_two = down_bank.shape[2]
    params = pltpu.CompilerParams(vmem_limit_bytes=VMEM_BYTES)

    def permute(x, route, name):
        with jax.named_scope(name):
            return lax.ppermute(x, "seq", route)

    def swap(x, name):
        with jax.named_scope(name + "_swap"):
            return lax.ppermute(x, "head", [(0, 1), (1, 0)])

    a0 = frames
    b0 = swap(a0, "own")
    q = pl.pallas_call(
        query_kernel,
        out_shape=jax.ShapeDtypeStruct((columns, rows), BF16),
        in_specs=[VMEM()] * 5,
        out_specs=VMEM(),
        compiler_params=params,
        cost_estimate=cost(10),
    )(a0, b0, w_query, w_key, w_value)
    near = [(i, i ^ 1) for i in range(count)]
    two = [(i, (i + 2) % count) for i in range(count)]
    rest = [(i, i + 1) for i in range(1, count - 1, 2)]

    a2 = permute(a0, two, "two")
    b2 = swap(a2, "two")
    a1 = permute(a0, near, "near")
    packed = down_bank.shape[1] % 32 == 0 and up_bank.shape[1] % 16 == 0
    reaching, *sent = rules(
        packed, bank_row, lang_ids, seg_ids, lookback, down_bank, up_bank, count
    )
    if packed:
        got = lax.all_to_all(sent[0], "seq", split_axis=0, concat_axis=0, tiled=True)
        half = pl.pallas_call(
            lower_kernel,
            out_shape=jax.ShapeDtypeStruct((count, down_bank.shape[1] // 2, LANES), BF16),
            in_specs=[VMEM()] * 3,
            out_specs=VMEM(),
            compiler_params=params,
        )(got, b2, q)
        other = swap(half, "down")
    else:
        wanted = jnp.take(bank_row, lang_ids, axis=0)
        got = lax.all_to_all(
            jnp.take(down_bank, wanted, axis=0), "seq", split_axis=0, concat_axis=0, tiled=True
        ).reshape(model_width, rank_two)
        other = lax.all_to_all(
            jnp.take(up_bank, wanted, axis=0), "seq", split_axis=0, concat_axis=0, tiled=True
        ).reshape(rank_two, columns)
    ax = permute(a2, near, "cross")
    a3 = permute(a2, rest, "rest")
    b1 = swap(a1, "near")

    state = (
        jax.ShapeDtypeStruct((heads, HD + 8, rows), F32),
        jax.ShapeDtypeStruct((heads, rows), F32),
    )
    weights = pltpu.VMEM((heads, rows, rows), BF16)
    half_frames = pltpu.VMEM((rows, width), BF16)
    acc, top, down, up, reached = pl.pallas_call(
        functools.partial(opening_kernel, packed),
        out_shape=state
        + (
            jax.ShapeDtypeStruct((model_width, rank_two), BF16),
            jax.ShapeDtypeStruct((rank_two, columns), BF16),
            jax.ShapeDtypeStruct((8, LANES), jnp.int32),
        ),
        in_specs=[VMEM()] * 5 + [HBM()] * 4 + [VMEM()] * 3,
        out_specs=(VMEM(),) * 5,
        scratch_shapes=[half_frames] * 4 + [weights, pltpu.SemaphoreType.DMA((4,))],
        compiler_params=params,
        cost_estimate=cost(0.1),
    )(
        got, other, reaching, a0, b0,
        *(pltpu.with_memory_space_constraint(x, pltpu.HBM) for x in (a2, b2, a1, b1)),
        q, w_key, w_value,
    )
    never = LOOK + 1
    ax, a3, reached = lax.optimization_barrier((ax, a3, reached))
    bx, b3 = swap(ax, "cross"), swap(a3, "rest")
    acc, top = pl.pallas_call(
        functools.partial(block_kernel, (1, 3)),
        out_shape=state,
        in_specs=[VMEM()] * 10,
        out_specs=(VMEM(), VMEM()),
        scratch_shapes=[weights],
        input_output_aliases={8: 0, 9: 1},
        compiler_params=params,
        cost_estimate=cost(2),
    )(reached, ax, bx, q, w_key, w_value, down, up, acc, top)
    return pl.pallas_call(
        functools.partial(closing_kernel, (3, never)),
        out_shape=jax.ShapeDtypeStruct((rows, columns), BF16),
        in_specs=[VMEM()] * 10,
        out_specs=VMEM(),
        scratch_shapes=[pltpu.VMEM(s.shape, F32) for s in state] + [weights],
        compiler_params=params,
        cost_estimate=cost(2),
    )(reached, a3, b3, q, w_key, w_value, down, up, acc, top)


def solution(mesh):
    in_specs = (
        P(("parts", "seq"), "head"),
        P(None, "head"),
        P(None, "head"),
        P(None, "head"),
        P(None, "seq", None),
        P(None, "seq", "head"),
        P(),
        P("parts"),
        P("parts"),
        P("parts"),
    )
    out_specs = P(("parts", "seq"), "head")
    return jax.shard_map(body, mesh=mesh, in_specs=in_specs, out_specs=out_specs, check_vma=False)
```

```python
import functools

import jax
import jax.numpy as jnp
from jax import lax
from jax.experimental import pallas as pl
from jax.experimental.pallas import tpu as pltpu
from jax.sharding import PartitionSpec as P

HD = 64
LANES = 128
LOOK = 3
VMEM_BYTES = 8 * 1024 * 1024
F32 = jnp.float32
BF16 = jnp.bfloat16

VMEM = functools.partial(pl.BlockSpec, memory_space=pltpu.VMEM)
ANY = functools.partial(pl.BlockSpec, memory_space=pl.ANY)
HBM = functools.partial(pl.BlockSpec, memory_space=pltpu.HBM)


def mm(a, b):
    return jnp.dot(a, b, preferred_element_type=F32)


def reach(seg_ref, look_ref, position):
    count = jnp.int32(0)
    for distance in range(1, LOOK + 1):
        earlier = jnp.maximum(position - distance, 0)
        allowed = (
            (position >= distance)
            & (look_ref[position] >= distance)
            & (seg_ref[earlier] == seg_ref[position])
        )
        count = count + allowed.astype(jnp.int32)
    return count


def rules_kernel(
    packed, row_hbm, lang_hbm, seg_hbm, look_hbm, down_hbm, up_hbm, *refs
):
    if packed:
        reach_ref, out_ref, row, lang, seg, look, down, up, sems = refs
        pairs = [(row_hbm, row), (lang_hbm, lang), (seg_hbm, seg), (look_hbm, look)]
        pairs += [(down_hbm, down), (up_hbm, up)]
    else:
        reach_ref, seg, look, sems = refs
        pairs = [(seg_hbm, seg), (look_hbm, look)]
    copies = [pltpu.make_async_copy(a, b, sems.at[k]) for k, (a, b) in enumerate(pairs)]
    for copy in copies:
        copy.start()
    for copy in copies:
        copy.wait()
    count = reach(seg, look, lax.axis_index("seq"))
    reach_ref[...] = jnp.full(reach_ref.shape, count, jnp.int32)
    if packed:
        half = down.shape[1] // 2
        depth = up.shape[1]
        mine = pl.ds(pl.multiple_of(lax.axis_index("head") * half, half), half)
        for j in range(out_ref.shape[0]):
            chosen = row[lang[j]]
            out_ref[j, :half, :] = down[chosen, mine, :]
            for c in range(up.shape[2] // LANES):
                out_ref[j, half + c * depth : half + (c + 1) * depth, :] = up[
                    chosen, :, c * LANES : (c + 1) * LANES
                ]


def cost(microseconds):
    return pl.CostEstimate(flops=int(microseconds * 1e9), bytes_accessed=0, transcendentals=0)


def rules(packed, bank_row, lang_ids, seg_ids, lookback, down_bank, up_bank, count):
    rows = down_bank.shape[1] // 2 + up_bank.shape[1] * (up_bank.shape[2] // LANES)
    out_shape = [jax.ShapeDtypeStruct((8, LANES), jnp.int32)]
    tables = [seg_ids, lookback]
    scratch = []
    if packed:
        out_shape.append(jax.ShapeDtypeStruct((count, rows, LANES), BF16))
        tables = [bank_row, lang_ids] + tables
        scratch = [pltpu.VMEM(down_bank.shape, BF16), pltpu.VMEM(up_bank.shape, BF16)]
    scratch = [pltpu.SMEM(t.shape, jnp.int32) for t in tables] + scratch
    return pl.pallas_call(
        functools.partial(rules_kernel, packed),
        out_shape=out_shape,
        in_specs=[HBM()] * 6,
        out_specs=[VMEM()] * len(out_shape),
        scratch_shapes=scratch + [pltpu.SemaphoreType.DMA((len(scratch),))],
        compiler_params=pltpu.CompilerParams(vmem_limit_bytes=VMEM_BYTES),
        cost_estimate=cost(2),
    )(
        *(
            pltpu.with_memory_space_constraint(x, pltpu.HBM)
            for x in (bank_row, lang_ids, seg_ids, lookback, down_bank, up_bank)
        )
    )


def halves(head, width):
    mine = pl.ds(pl.multiple_of(head * width, width), width)
    other = pl.ds(pl.multiple_of((1 - head) * width, width), width)
    return mine, other


def query_kernel(a, b, wq, wk, wv, q_ref):
    mine, other = halves(lax.axis_index("head"), a.shape[1])
    queries = (mm(a[...], wq[mine, :]) + mm(b[...], wq[other, :])).astype(BF16)
    q_ref[...] = (queries * jnp.asarray(HD**-0.5, BF16)).T


def lower_kernel(got, b_ref, q_ref, reach_ref, half_ref, token_ref):
    token_ref[...] = reach_ref[...]
    half_ref[...] = got[:, : half_ref.shape[1], :]


def unpack(got, other, down_ref, up_ref):
    head = lax.axis_index("head")
    half = other.shape[1]
    depth = up_ref.shape[0] // got.shape[0]
    for j in range(got.shape[0]):
        for part, source in ((head, got), (1 - head, other)):
            place = pl.ds(pl.multiple_of(j * 2 * half + part * half, half), half)
            down_ref[place, :] = source[j, :half, :]
    for c in range(up_ref.shape[1] // LANES):
        piece = got[:, half + c * depth : half + (c + 1) * depth, :]
        up_ref[:, c * LANES : (c + 1) * LANES] = piece.reshape(up_ref.shape[0], LANES)


def keys_values(a, b, wk, wv, down_ref, up_ref):
    mine, other = halves(lax.axis_index("head"), a.shape[1])
    first, second = a[...], b[...]
    lowrank = mm(first, down_ref[mine, :]) + mm(second, down_ref[other, :])
    lowrank = lowrank.astype(BF16)
    lane = lax.broadcasted_iota(jnp.int32, lowrank.shape, 1)
    split = lowrank.shape[1] // 2
    zero = jnp.zeros_like(lowrank)
    low_key = jnp.where(lane < split, lowrank, zero)
    low_value = jnp.where(lane < split, zero, lowrank)
    up = up_ref[...]
    keys = mm(first, wk[mine, :]) + mm(second, wk[other, :]) + mm(low_key, up)
    values = mm(first, wv[mine, :]) + mm(second, wv[other, :]) + mm(low_value, up)
    return keys.astype(BF16), values.astype(BF16)


def attend(q_ref, keys, values, before, after, weights_ref):
    turned = values.T
    ones = jnp.ones((16, turned.shape[1]), BF16)
    acc_ref, max_ref = after
    heads = acc_ref.shape[0]
    factors = []
    for i in range(heads):
        q = q_ref[i * HD : (i + 1) * HD, :]
        zero = jnp.zeros_like(q)
        q = jnp.concatenate([q, zero] if i % 2 == 0 else [zero, q], axis=0)
        scores = mm(keys[:, i // 2 * LANES : (i // 2 + 1) * LANES], q)
        top = jnp.max(scores, axis=0, keepdims=True)
        if before is not None:
            old = before[1][i : i + 1, :]
            top = jnp.maximum(top, old)
            factors.append(jnp.exp(old - top))
        weights_ref[i] = jnp.exp(scores - top).astype(BF16)
        max_ref[i : i + 1, :] = top
    for i in range(heads):
        left = jnp.concatenate([turned[i * HD : (i + 1) * HD, :], ones], axis=0)
        update = mm(left, weights_ref[i])[: acc_ref.shape[1], :]
        if before is not None:
            update = before[0][i] * factors[i] + update
        acc_ref[i] = update


def finish(acc_ref, out_ref):
    for pair in range(acc_ref.shape[0] // 2):
        parts = []
        for i in (2 * pair, 2 * pair + 1):
            parts.append(acc_ref[i, :HD, :] / acc_ref[i, HD : HD + 1, :])
        out_ref[:, pair * LANES : (pair + 1) * LANES] = (
            jnp.concatenate(parts, axis=0).T.astype(BF16)
        )


def opening_kernel(
    packed, got, other, reach_ref, a0, b0, a2_hbm, b2_hbm, a1_hbm, b1_hbm, q_ref, wk, wv,
    acc_ref, max_ref, down_ref, up_ref, token_ref, a2, b2, a1, b1, weights_ref, sems,
):
    pairs = ((a2_hbm, a2), (b2_hbm, b2), (a1_hbm, a1), (b1_hbm, b1))
    copies = [pltpu.make_async_copy(x, y, sems.at[k]) for k, (x, y) in enumerate(pairs)]
    for copy in copies:
        copy.start()
    token_ref[...] = reach_ref[...]
    if packed:
        unpack(got, other, down_ref, up_ref)
    else:
        down_ref[...] = got[...]
        up_ref[...] = other[...]
    state = (acc_ref, max_ref)
    keys, values = keys_values(a0, b0, wk, wv, down_ref, up_ref)
    attend(q_ref, keys, values, None, state, weights_ref)
    for copy in copies:
        copy.wait()
    count = reach_ref[0, 0]

    @pl.when(count >= 2)
    def _():
        keys, values = keys_values(a2, b2, wk, wv, down_ref, up_ref)
        attend(q_ref, keys, values, state, state, weights_ref)

    @pl.when((lax.axis_index("seq") % 2 == 1) & (count >= 1))
    def _():
        keys, values = keys_values(a1, b1, wk, wv, down_ref, up_ref)
        attend(q_ref, keys, values, state, state, weights_ref)


def block_kernel(
    distances, reach_ref, a, b, q_ref, wk, wv, down_ref, up_ref, acc_in, max_in,
    acc_ref, max_ref, token_ref, weights_ref,
):
    odd = lax.axis_index("seq") % 2
    even_distance, odd_distance = distances
    distance = jnp.where(odd == 1, odd_distance, even_distance)
    token_ref[...] = reach_ref[...]

    @pl.when(reach_ref[0, 0] >= distance)
    def _():
        keys, values = keys_values(a, b, wk, wv, down_ref, up_ref)
        attend(q_ref, keys, values, (acc_in, max_in), (acc_ref, max_ref), weights_ref)


def closing_kernel(
    distances, reach_ref, a, b, q_ref, wk, wv, down_ref, up_ref, acc_in, max_in,
    out_ref, acc_ref, max_ref, weights_ref,
):
    odd = lax.axis_index("seq") % 2
    even_distance, odd_distance = distances
    distance = jnp.where(odd == 1, odd_distance, even_distance)
    needed = reach_ref[0, 0] >= distance

    @pl.when(needed)
    def _():
        keys, values = keys_values(a, b, wk, wv, down_ref, up_ref)
        attend(q_ref, keys, values, (acc_in, max_in), (acc_ref, max_ref), weights_ref)
        finish(acc_ref, out_ref)

    @pl.when(jnp.logical_not(needed))
    def _():
        finish(acc_in, out_ref)


def body(
    frames, w_query, w_key, w_value, down_bank, up_bank, bank_row, lang_ids, seg_ids, lookback
):
    count = lax.axis_size("seq")
    rows, width = frames.shape
    columns = w_query.shape[1]
    heads = columns // HD
    model_width = w_query.shape[0]
    rank_two = down_bank.shape[2]
    params = pltpu.CompilerParams(vmem_limit_bytes=VMEM_BYTES)

    def permute(x, route, name):
        with jax.named_scope(name):
            return lax.ppermute(x, "seq", route)

    def swap(x, name):
        with jax.named_scope(name + "_swap"):
            return lax.ppermute(x, "head", [(0, 1), (1, 0)])

    a0 = frames
    b0 = swap(a0, "own")
    q = pl.pallas_call(
        query_kernel,
        out_shape=jax.ShapeDtypeStruct((columns, rows), BF16),
        in_specs=[VMEM()] * 5,
        out_specs=VMEM(),
        compiler_params=params,
        cost_estimate=cost(10),
    )(a0, b0, w_query, w_key, w_value)
    near = [(i, i ^ 1) for i in range(count)]
    two = [(i, (i + 2) % count) for i in range(count)]
    pairs = [(0, 0), (count - 1, count - 1)]
    pairs += [(i, i + 1 if i % 2 else i - 1) for i in range(1, count - 1)]

    a2 = permute(a0, two, "two")
    b2 = swap(a2, "two")
    a1 = permute(a0, near, "near")
    packed = down_bank.shape[1] % 32 == 0 and up_bank.shape[1] % 16 == 0
    reaching, *sent = rules(
        packed, bank_row, lang_ids, seg_ids, lookback, down_bank, up_bank, count
    )
    if packed:
        got = lax.all_to_all(sent[0], "seq", split_axis=0, concat_axis=0, tiled=True)
        half, reaching = pl.pallas_call(
            lower_kernel,
            out_shape=(
                jax.ShapeDtypeStruct((count, down_bank.shape[1] // 2, LANES), BF16),
                jax.ShapeDtypeStruct((8, LANES), jnp.int32),
            ),
            in_specs=[VMEM()] * 4,
            out_specs=(VMEM(), VMEM()),
            compiler_params=params,
        )(got, b2, q, reaching)
        other = swap(half, "down")
    else:
        wanted = jnp.take(bank_row, lang_ids, axis=0)
        got = lax.all_to_all(
            jnp.take(down_bank, wanted, axis=0), "seq", split_axis=0, concat_axis=0, tiled=True
        ).reshape(model_width, rank_two)
        other = lax.all_to_all(
            jnp.take(up_bank, wanted, axis=0), "seq", split_axis=0, concat_axis=0, tiled=True
        ).reshape(rank_two, columns)
    moved = jnp.where(lax.axis_index("head") == 0, a2, a1)
    ways = [(2 * i, 2 * j) for i, j in near] + [(2 * i + 1, 2 * j + 1) for i, j in two]
    with jax.named_scope("split"):
        ax = lax.ppermute(moved, ("seq", "head"), ways)
    a3 = permute(a2, pairs, "rest")
    ax, reaching = lax.optimization_barrier((ax, reaching))
    b1, bx = swap(a1, "near"), swap(ax, "cross")

    state = (
        jax.ShapeDtypeStruct((heads, HD + 8, rows), F32),
        jax.ShapeDtypeStruct((heads, rows), F32),
    )
    weights = pltpu.VMEM((heads, rows, rows), BF16)
    half_frames = pltpu.VMEM((rows, width), BF16)
    acc, top, down, up, reached = pl.pallas_call(
        functools.partial(opening_kernel, packed),
        out_shape=state
        + (
            jax.ShapeDtypeStruct((model_width, rank_two), BF16),
            jax.ShapeDtypeStruct((rank_two, columns), BF16),
            jax.ShapeDtypeStruct((8, LANES), jnp.int32),
        ),
        in_specs=[VMEM()] * 5 + [ANY()] * 4 + [VMEM()] * 3,
        out_specs=(VMEM(),) * 5,
        scratch_shapes=[half_frames] * 4 + [weights, pltpu.SemaphoreType.DMA((4,))],
        compiler_params=params,
        cost_estimate=cost(0.1),
    )(
        got, other, reaching, a0, b0,
        *(x for x in (a2, b2, a1, b1)),
        q, w_key, w_value,
    )
    never = LOOK + 1
    a3, reached = lax.optimization_barrier((a3, reached))
    acc, top, reached = pl.pallas_call(
        functools.partial(block_kernel, (1, 3)),
        out_shape=state + (jax.ShapeDtypeStruct((8, LANES), jnp.int32),),
        in_specs=[VMEM()] * 10,
        out_specs=(VMEM(),) * 3,
        scratch_shapes=[weights],
        input_output_aliases={8: 0, 9: 1},
        compiler_params=params,
        cost_estimate=cost(0.1),
    )(reached, ax, bx, q, w_key, w_value, down, up, acc, top)
    b3 = swap(a3, "rest")
    return pl.pallas_call(
        functools.partial(closing_kernel, (3, never)),
        out_shape=jax.ShapeDtypeStruct((rows, columns), BF16),
        in_specs=[VMEM()] * 10,
        out_specs=VMEM(),
        scratch_shapes=[pltpu.VMEM(s.shape, F32) for s in state] + [weights],
        compiler_params=params,
        cost_estimate=cost(2),
    )(reached, a3, b3, q, w_key, w_value, down, up, acc, top)


def solution(mesh):
    in_specs = (
        P(("parts", "seq"), "head"),
        P(None, "head"),
        P(None, "head"),
        P(None, "head"),
        P(None, "seq", None),
        P(None, "seq", "head"),
        P(),
        P("parts"),
        P("parts"),
        P("parts"),
    )
    out_specs = P(("parts", "seq"), "head")
    return jax.shard_map(body, mesh=mesh, in_specs=in_specs, out_specs=out_specs, check_vma=False)
```

```python
import functools

import jax
import jax.numpy as jnp
from jax import lax
from jax.experimental import pallas as pl
from jax.experimental.pallas import tpu as pltpu
from jax.sharding import PartitionSpec as P

HD = 64
LANES = 128
LOOK = 3
VMEM_BYTES = 8 * 1024 * 1024
F32 = jnp.float32
BF16 = jnp.bfloat16

VMEM = functools.partial(pl.BlockSpec, memory_space=pltpu.VMEM)
ANY = functools.partial(pl.BlockSpec, memory_space=pl.ANY)
HBM = functools.partial(pl.BlockSpec, memory_space=pltpu.HBM)


def mm(a, b):
    return jnp.dot(a, b, preferred_element_type=F32)


def reach(seg_ref, look_ref, position):
    count = jnp.int32(0)
    for distance in range(1, LOOK + 1):
        earlier = jnp.maximum(position - distance, 0)
        allowed = (
            (position >= distance)
            & (look_ref[position] >= distance)
            & (seg_ref[earlier] == seg_ref[position])
        )
        count = count + allowed.astype(jnp.int32)
    return count


def rules_kernel(
    packed, row_hbm, lang_hbm, seg_hbm, look_hbm, down_hbm, up_hbm, *refs
):
    if packed:
        reach_ref, out_ref, row, lang, seg, look, down, up, sems = refs
        pairs = [(row_hbm, row), (lang_hbm, lang), (seg_hbm, seg), (look_hbm, look)]
        pairs += [(down_hbm, down), (up_hbm, up)]
    else:
        reach_ref, seg, look, sems = refs
        pairs = [(seg_hbm, seg), (look_hbm, look)]
    copies = [pltpu.make_async_copy(a, b, sems.at[k]) for k, (a, b) in enumerate(pairs)]
    for copy in copies:
        copy.start()
    for copy in copies:
        copy.wait()
    count = reach(seg, look, lax.axis_index("seq"))
    reach_ref[...] = jnp.full(reach_ref.shape, count, jnp.int32)
    if packed:
        half = down.shape[1] // 2
        depth = up.shape[1]
        mine = pl.ds(pl.multiple_of(lax.axis_index("head") * half, half), half)
        for j in range(out_ref.shape[0]):
            chosen = row[lang[j]]
            out_ref[j, :half, :] = down[chosen, mine, :]
            for c in range(up.shape[2] // LANES):
                out_ref[j, half + c * depth : half + (c + 1) * depth, :] = up[
                    chosen, :, c * LANES : (c + 1) * LANES
                ]


def cost(microseconds):
    return pl.CostEstimate(flops=int(microseconds * 1e9), bytes_accessed=0, transcendentals=0)


def rules(packed, bank_row, lang_ids, seg_ids, lookback, down_bank, up_bank, count):
    rows = down_bank.shape[1] // 2 + up_bank.shape[1] * (up_bank.shape[2] // LANES)
    out_shape = [jax.ShapeDtypeStruct((8, LANES), jnp.int32)]
    tables = [seg_ids, lookback]
    scratch = []
    if packed:
        out_shape.append(jax.ShapeDtypeStruct((count, rows, LANES), BF16))
        tables = [bank_row, lang_ids] + tables
        scratch = [pltpu.VMEM(down_bank.shape, BF16), pltpu.VMEM(up_bank.shape, BF16)]
    scratch = [pltpu.SMEM(t.shape, jnp.int32) for t in tables] + scratch
    return pl.pallas_call(
        functools.partial(rules_kernel, packed),
        out_shape=out_shape,
        in_specs=[HBM()] * 6,
        out_specs=[VMEM()] * len(out_shape),
        scratch_shapes=scratch + [pltpu.SemaphoreType.DMA((len(scratch),))],
        compiler_params=pltpu.CompilerParams(vmem_limit_bytes=VMEM_BYTES),
        cost_estimate=cost(2),
    )(
        *(
            pltpu.with_memory_space_constraint(x, pltpu.HBM)
            for x in (bank_row, lang_ids, seg_ids, lookback, down_bank, up_bank)
        )
    )


def halves(head, width):
    mine = pl.ds(pl.multiple_of(head * width, width), width)
    other = pl.ds(pl.multiple_of((1 - head) * width, width), width)
    return mine, other


def query_kernel(a, b, wq, q_ref):
    mine, other = halves(lax.axis_index("head"), a.shape[1])
    queries = (mm(a[...], wq[mine, :]) + mm(b[...], wq[other, :])).astype(BF16)
    q_ref[...] = (queries * jnp.asarray(HD**-0.5, BF16)).T


def lower_kernel(got, b_ref, q_ref, reach_ref, wk, wv, half_ref, token_ref):
    token_ref[...] = reach_ref[...]
    half_ref[...] = got[:, : half_ref.shape[1], :]


def unpack(got, other, down_ref, up_ref):
    head = lax.axis_index("head")
    half = other.shape[1]
    depth = up_ref.shape[0] // got.shape[0]
    for j in range(got.shape[0]):
        for part, source in ((head, got), (1 - head, other)):
            place = pl.ds(pl.multiple_of(j * 2 * half + part * half, half), half)
            down_ref[place, :] = source[j, :half, :]
    for c in range(up_ref.shape[1] // LANES):
        piece = got[:, half + c * depth : half + (c + 1) * depth, :]
        up_ref[:, c * LANES : (c + 1) * LANES] = piece.reshape(up_ref.shape[0], LANES)


def project(a, b, wk, wv, down_ref, up_ref, keys_ref, turned_ref):
    mine, other = halves(lax.axis_index("head"), a.shape[1])
    first, second = a[...], b[...]
    lowrank = mm(first, down_ref[mine, :]) + mm(second, down_ref[other, :])
    lowrank = lowrank.astype(BF16)
    lane = lax.broadcasted_iota(jnp.int32, lowrank.shape, 1)
    split = lowrank.shape[1] // 2
    zero = jnp.zeros_like(lowrank)
    low_key = jnp.where(lane < split, lowrank, zero)
    low_value = jnp.where(lane < split, zero, lowrank)
    up = up_ref[...]
    keys = mm(first, wk[mine, :]) + mm(second, wk[other, :]) + mm(low_key, up)
    values = mm(first, wv[mine, :]) + mm(second, wv[other, :]) + mm(low_value, up)
    keys_ref[...] = keys.astype(BF16)
    turned_ref[...] = values.astype(BF16).T


def attend(q_ref, keys_ref, turned_ref, before, after, weights_ref):
    keys = keys_ref[...]
    ones = jnp.ones((16, turned_ref.shape[1]), BF16)
    acc_ref, max_ref = after
    heads = acc_ref.shape[0]
    factors = []
    for i in range(heads):
        q = q_ref[i * HD : (i + 1) * HD, :]
        zero = jnp.zeros_like(q)
        q = jnp.concatenate([q, zero] if i % 2 == 0 else [zero, q], axis=0)
        scores = mm(keys[:, i // 2 * LANES : (i // 2 + 1) * LANES], q)
        top = jnp.max(scores, axis=0, keepdims=True)
        if before is not None:
            old = before[1][i : i + 1, :]
            top = jnp.maximum(top, old)
            factors.append(jnp.exp(old - top))
        weights_ref[i] = jnp.exp(scores - top).astype(BF16)
        max_ref[i : i + 1, :] = top
    for i in range(heads):
        left = jnp.concatenate([turned_ref[i * HD : (i + 1) * HD, :], ones], axis=0)
        update = mm(left, weights_ref[i])[: acc_ref.shape[1], :]
        if before is not None:
            update = before[0][i] * factors[i] + update
        acc_ref[i] = update


def loads(pairs, sems):
    copies = [pltpu.make_async_copy(x, y, sems.at[k]) for k, (x, y) in enumerate(pairs)]

    def start():
        for copy in copies:
            copy.start()

    def wait():
        for copy in copies:
            copy.wait()

    return start, wait


def finish(acc_ref, out_ref):
    for pair in range(acc_ref.shape[0] // 2):
        parts = []
        for i in (2 * pair, 2 * pair + 1):
            parts.append(acc_ref[i, :HD, :] / acc_ref[i, HD : HD + 1, :])
        out_ref[:, pair * LANES : (pair + 1) * LANES] = (
            jnp.concatenate(parts, axis=0).T.astype(BF16)
        )


def opening_kernel(
    packed, got, other, reach_ref, a0, b0, a2_any, b2_any, a1_any, b1_any, q_ref, wk, wv,
    acc_ref, max_ref, keys_ref, turned_ref, down_ref, up_ref, token_ref,
    a2, b2, a1, b1, weights_ref, sems,
):
    count = reach_ref[0, 0]
    odd = lax.axis_index("seq") % 2 == 1
    start, wait = loads(((a2_any, a2), (b2_any, b2), (a1_any, a1), (b1_any, b1)), sems)
    start()
    token_ref[...] = reach_ref[...]
    if packed:
        unpack(got, other, down_ref, up_ref)
    else:
        down_ref[...] = got[...]
        up_ref[...] = other[...]
    state = (acc_ref, max_ref)
    project(a0, b0, wk, wv, down_ref, up_ref, keys_ref, turned_ref)
    attend(q_ref, keys_ref, turned_ref, None, state, weights_ref)
    wait()

    @pl.when(count >= 2)
    def _():
        project(a2, b2, wk, wv, down_ref, up_ref, keys_ref, turned_ref)

    @pl.when(odd & (count >= 2))
    def _():
        attend(q_ref, keys_ref, turned_ref, state, state, weights_ref)

    @pl.when(odd & (count >= 1))
    def _():
        project(a1, b1, wk, wv, down_ref, up_ref, keys_ref, turned_ref)


def middle_kernel(
    reach_ref, ax_any, bx_any, q_ref, wk, wv, down_ref, up_ref, acc_in, max_in, keys_in, turned_in,
    acc_ref, max_ref, keys_ref, turned_ref, token_ref, a, b, weights_ref, sems,
):
    count = reach_ref[0, 0]
    odd = lax.axis_index("seq") % 2 == 1
    needed = count >= jnp.where(odd, 3, 1)
    start, wait = loads(((ax_any, a), (bx_any, b)), sems)
    pl.when(needed)(start)
    token_ref[...] = reach_ref[...]

    @pl.when(count >= jnp.where(odd, 1, 2))
    def _():
        attend(q_ref, keys_in, turned_in, (acc_in, max_in), (acc_ref, max_ref), weights_ref)

    @pl.when(needed)
    def _():
        wait()
        project(a, b, wk, wv, down_ref, up_ref, keys_ref, turned_ref)


def closing_kernel(
    reach_ref, a3_any, b3_any, q_ref, wk, wv, down_ref, up_ref, acc_in, max_in, keys_in, turned_in,
    out_ref, acc_ref, max_ref, keys_ref, turned_ref, a, b, weights_ref, sems,
):
    count = reach_ref[0, 0]
    odd = lax.axis_index("seq") % 2 == 1
    pending = count >= jnp.where(odd, 3, 1)
    needed = (count >= 3) & jnp.logical_not(odd)
    start, wait = loads(((a3_any, a), (b3_any, b)), sems)
    state = (acc_ref, max_ref)
    pl.when(needed)(start)

    @pl.when(pending)
    def _():
        attend(q_ref, keys_in, turned_in, (acc_in, max_in), state, weights_ref)

        @pl.when(needed)
        def _():
            wait()
            project(a, b, wk, wv, down_ref, up_ref, keys_ref, turned_ref)
            attend(q_ref, keys_ref, turned_ref, state, state, weights_ref)

        finish(acc_ref, out_ref)

    @pl.when(jnp.logical_not(pending))
    def _():
        finish(acc_in, out_ref)


def body(
    frames, w_query, w_key, w_value, down_bank, up_bank, bank_row, lang_ids, seg_ids, lookback
):
    count = lax.axis_size("seq")
    rows, width = frames.shape
    columns = w_query.shape[1]
    heads = columns // HD
    model_width = w_query.shape[0]
    rank_two = down_bank.shape[2]
    params = pltpu.CompilerParams(vmem_limit_bytes=VMEM_BYTES)

    def permute(x, route, name):
        with jax.named_scope(name):
            return lax.ppermute(x, "seq", route)

    def swap(x, name):
        with jax.named_scope(name + "_swap"):
            return lax.ppermute(x, "head", [(0, 1), (1, 0)])

    a0 = frames
    b0 = swap(a0, "own")
    q = pl.pallas_call(
        query_kernel,
        out_shape=jax.ShapeDtypeStruct((columns, rows), BF16),
        in_specs=[VMEM()] * 3,
        out_specs=VMEM(),
        compiler_params=params,
        cost_estimate=cost(10),
    )(a0, b0, w_query)
    near = [(i, i ^ 1) for i in range(count)]
    two = [(i, (i + 2) % count) for i in range(count)]
    pairs = [(0, 0), (count - 1, count - 1)]
    pairs += [(i, i + 1 if i % 2 else i - 1) for i in range(1, count - 1)]

    a2 = permute(a0, two, "two")
    b2 = swap(a2, "two")
    a1 = permute(a0, near, "near")
    packed = down_bank.shape[1] % 32 == 0 and up_bank.shape[1] % 16 == 0
    reaching, *sent = rules(
        packed, bank_row, lang_ids, seg_ids, lookback, down_bank, up_bank, count
    )
    if packed:
        got = lax.all_to_all(sent[0], "seq", split_axis=0, concat_axis=0, tiled=True)
        half, reaching = pl.pallas_call(
            lower_kernel,
            out_shape=(
                jax.ShapeDtypeStruct((count, down_bank.shape[1] // 2, LANES), BF16),
                jax.ShapeDtypeStruct((8, LANES), jnp.int32),
            ),
            in_specs=[VMEM()] * 6,
            out_specs=(VMEM(), VMEM()),
            compiler_params=params,
        )(got, b2, q, reaching, w_key, w_value)
        other = swap(half, "down")
    else:
        wanted = jnp.take(bank_row, lang_ids, axis=0)
        got = lax.all_to_all(
            jnp.take(down_bank, wanted, axis=0), "seq", split_axis=0, concat_axis=0, tiled=True
        ).reshape(model_width, rank_two)
        other = lax.all_to_all(
            jnp.take(up_bank, wanted, axis=0), "seq", split_axis=0, concat_axis=0, tiled=True
        ).reshape(rank_two, columns)
    moved = jnp.where(lax.axis_index("head") == 0, a2, a1)
    ways = [(2 * i, 2 * j) for i, j in near] + [(2 * i + 1, 2 * j + 1) for i, j in two]
    with jax.named_scope("split"):
        ax = lax.ppermute(moved, ("seq", "head"), ways)
    a3 = permute(a2, pairs, "rest")
    ax, reaching = lax.optimization_barrier((ax, reaching))
    b1, bx = swap(a1, "near"), swap(ax, "cross")

    state = (
        jax.ShapeDtypeStruct((heads, HD + 8, rows), F32),
        jax.ShapeDtypeStruct((heads, rows), F32),
    )
    weights = pltpu.VMEM((heads, rows, rows), BF16)
    half_frames = pltpu.VMEM((rows, width), BF16)
    projected = (
        jax.ShapeDtypeStruct((rows, columns), BF16),
        jax.ShapeDtypeStruct((columns, rows), BF16),
    )
    token = jax.ShapeDtypeStruct((8, LANES), jnp.int32)
    acc, top, keys, turned, down, up, reached = pl.pallas_call(
        functools.partial(opening_kernel, packed),
        out_shape=state
        + projected
        + (
            jax.ShapeDtypeStruct((model_width, rank_two), BF16),
            jax.ShapeDtypeStruct((rank_two, columns), BF16),
            token,
        ),
        in_specs=[VMEM()] * 5 + [ANY()] * 4 + [VMEM()] * 3,
        out_specs=(VMEM(),) * 7,
        scratch_shapes=[half_frames] * 4 + [weights, pltpu.SemaphoreType.DMA((4,))],
        compiler_params=params,
        cost_estimate=cost(0.1),
    )(got, other, reaching, a0, b0, a2, b2, a1, b1, q, w_key, w_value)
    a3, reached = lax.optimization_barrier((a3, reached))
    acc, top, keys, turned, reached = pl.pallas_call(
        middle_kernel,
        out_shape=state + projected + (token,),
        in_specs=[VMEM()] + [ANY()] * 2 + [VMEM()] * 9,
        out_specs=(VMEM(),) * 5,
        scratch_shapes=[half_frames] * 2 + [weights, pltpu.SemaphoreType.DMA((2,))],
        input_output_aliases={8: 0, 9: 1},
        compiler_params=params,
        cost_estimate=cost(0.1),
    )(reached, ax, bx, q, w_key, w_value, down, up, acc, top, keys, turned)
    b3 = swap(a3, "rest")
    return pl.pallas_call(
        closing_kernel,
        out_shape=jax.ShapeDtypeStruct((rows, columns), BF16),
        in_specs=[VMEM()] + [ANY()] * 2 + [VMEM()] * 9,
        out_specs=VMEM(),
        scratch_shapes=[pltpu.VMEM(s.shape, s.dtype) for s in state + projected]
        + [half_frames] * 2
        + [weights, pltpu.SemaphoreType.DMA((2,))],
        compiler_params=params,
        cost_estimate=cost(2),
    )(reached, a3, b3, q, w_key, w_value, down, up, acc, top, keys, turned)


def solution(mesh):
    in_specs = (
        P(("parts", "seq"), "head"),
        P(None, "head"),
        P(None, "head"),
        P(None, "head"),
        P(None, "seq", None),
        P(None, "seq", "head"),
        P(),
        P("parts"),
        P("parts"),
        P("parts"),
    )
    out_specs = P(("parts", "seq"), "head")
    return jax.shard_map(body, mesh=mesh, in_specs=in_specs, out_specs=out_specs, check_vma=False)
```

```python
import functools

import jax
import jax.numpy as jnp
from jax import lax
from jax.experimental import pallas as pl
from jax.experimental.pallas import tpu as pltpu
from jax.sharding import PartitionSpec as P

HD = 64
LANES = 128
LOOK = 3
VMEM_BYTES = 8 * 1024 * 1024
F32 = jnp.float32
BF16 = jnp.bfloat16

VMEM = functools.partial(pl.BlockSpec, memory_space=pltpu.VMEM)
ANY = functools.partial(pl.BlockSpec, memory_space=pl.ANY)
HBM = functools.partial(pl.BlockSpec, memory_space=pltpu.HBM)


def mm(a, b):
    return jnp.dot(a, b, preferred_element_type=F32)


def reach(seg_ref, look_ref, position):
    count = jnp.int32(0)
    for distance in range(1, LOOK + 1):
        earlier = jnp.maximum(position - distance, 0)
        allowed = (
            (position >= distance)
            & (look_ref[position] >= distance)
            & (seg_ref[earlier] == seg_ref[position])
        )
        count = count + allowed.astype(jnp.int32)
    return count


def rules_kernel(
    packed, row_hbm, lang_hbm, seg_hbm, look_hbm, down_hbm, up_hbm, *refs
):
    if packed:
        reach_ref, out_ref, row, lang, seg, look, down, up, sems = refs
        pairs = [(row_hbm, row), (lang_hbm, lang), (seg_hbm, seg), (look_hbm, look)]
        pairs += [(down_hbm, down), (up_hbm, up)]
    else:
        reach_ref, seg, look, sems = refs
        pairs = [(seg_hbm, seg), (look_hbm, look)]
    copies = [pltpu.make_async_copy(a, b, sems.at[k]) for k, (a, b) in enumerate(pairs)]
    for copy in copies:
        copy.start()
    for copy in copies:
        copy.wait()
    count = reach(seg, look, lax.axis_index("seq"))
    reach_ref[...] = jnp.full(reach_ref.shape, count, jnp.int32)
    if packed:
        half = down.shape[1] // 2
        depth = up.shape[1]
        mine = pl.ds(pl.multiple_of(lax.axis_index("head") * half, half), half)
        for j in range(out_ref.shape[0]):
            chosen = row[lang[j]]
            out_ref[j, :half, :] = down[chosen, mine, :]
            for c in range(up.shape[2] // LANES):
                out_ref[j, half + c * depth : half + (c + 1) * depth, :] = up[
                    chosen, :, c * LANES : (c + 1) * LANES
                ]


def cost(microseconds):
    return pl.CostEstimate(flops=int(microseconds * 1e9), bytes_accessed=0, transcendentals=0)


def rules(packed, bank_row, lang_ids, seg_ids, lookback, down_bank, up_bank, count):
    rows = down_bank.shape[1] // 2 + up_bank.shape[1] * (up_bank.shape[2] // LANES)
    out_shape = [jax.ShapeDtypeStruct((8, LANES), jnp.int32)]
    tables = [seg_ids, lookback]
    scratch = []
    if packed:
        out_shape.append(jax.ShapeDtypeStruct((count, rows, LANES), BF16))
        tables = [bank_row, lang_ids] + tables
        scratch = [pltpu.VMEM(down_bank.shape, BF16), pltpu.VMEM(up_bank.shape, BF16)]
    scratch = [pltpu.SMEM(t.shape, jnp.int32) for t in tables] + scratch
    return pl.pallas_call(
        functools.partial(rules_kernel, packed),
        out_shape=out_shape,
        in_specs=[HBM()] * 6,
        out_specs=[VMEM()] * len(out_shape),
        scratch_shapes=scratch + [pltpu.SemaphoreType.DMA((len(scratch),))],
        compiler_params=pltpu.CompilerParams(vmem_limit_bytes=VMEM_BYTES),
        cost_estimate=cost(2),
    )(
        *(
            pltpu.with_memory_space_constraint(x, pltpu.HBM)
            for x in (bank_row, lang_ids, seg_ids, lookback, down_bank, up_bank)
        )
    )


def halves(head, width):
    mine = pl.ds(pl.multiple_of(head * width, width), width)
    other = pl.ds(pl.multiple_of((1 - head) * width, width), width)
    return mine, other


def query_kernel(a_hbm, b_hbm, wq_hbm, q_ref, b, a, wq, sems):
    pairs = ((a_hbm, a), (b_hbm, b), (wq_hbm, wq))
    copies = [pltpu.make_async_copy(x, y, sems.at[k]) for k, (x, y) in enumerate(pairs)]
    for copy in copies:
        copy.start()
    for copy in copies:
        copy.wait()
    mine, other = halves(lax.axis_index("head"), a.shape[1])
    queries = (mm(a[...], wq[mine, :]) + mm(b[...], wq[other, :])).astype(BF16)
    q_ref[...] = (queries * jnp.asarray(HD**-0.5, BF16)).T


def lower_kernel(got, q_ref, reach_ref, wk, wv, half_ref, token_ref):
    token_ref[...] = reach_ref[...]
    half_ref[...] = got[:, : half_ref.shape[1], :]


def unpack(got, other, down_ref, up_ref):
    head = lax.axis_index("head")
    half = other.shape[1]
    depth = up_ref.shape[0] // got.shape[0]
    for j in range(got.shape[0]):
        for part, source in ((head, got), (1 - head, other)):
            place = pl.ds(pl.multiple_of(j * 2 * half + part * half, half), half)
            down_ref[place, :] = source[j, :half, :]
    for c in range(up_ref.shape[1] // LANES):
        piece = got[:, half + c * depth : half + (c + 1) * depth, :]
        up_ref[:, c * LANES : (c + 1) * LANES] = piece.reshape(up_ref.shape[0], LANES)


def project(a, b, wk, wv, down_ref, up_ref, keys_ref, turned_ref):
    mine, other = halves(lax.axis_index("head"), a.shape[1])
    first, second = a[...], b[...]
    lowrank = mm(first, down_ref[mine, :]) + mm(second, down_ref[other, :])
    lowrank = lowrank.astype(BF16)
    lane = lax.broadcasted_iota(jnp.int32, lowrank.shape, 1)
    split = lowrank.shape[1] // 2
    zero = jnp.zeros_like(lowrank)
    low_key = jnp.where(lane < split, lowrank, zero)
    low_value = jnp.where(lane < split, zero, lowrank)
    up = up_ref[...]
    keys = mm(first, wk[mine, :]) + mm(second, wk[other, :]) + mm(low_key, up)
    values = mm(first, wv[mine, :]) + mm(second, wv[other, :]) + mm(low_value, up)
    keys_ref[...] = keys.astype(BF16)
    turned_ref[...] = values.astype(BF16).T


def attend(q_ref, keys_ref, turned_ref, before, after, weights_ref):
    keys = keys_ref[...]
    ones = jnp.ones((16, turned_ref.shape[1]), BF16)
    acc_ref, max_ref = after
    heads = acc_ref.shape[0]
    factors = []
    for i in range(heads):
        q = q_ref[i * HD : (i + 1) * HD, :]
        zero = jnp.zeros_like(q)
        q = jnp.concatenate([q, zero] if i % 2 == 0 else [zero, q], axis=0)
        scores = mm(keys[:, i // 2 * LANES : (i // 2 + 1) * LANES], q)
        top = jnp.max(scores, axis=0, keepdims=True)
        if before is not None:
            old = before[1][i : i + 1, :]
            top = jnp.maximum(top, old)
            factors.append(jnp.exp(old - top))
        weights_ref[i] = jnp.exp(scores - top).astype(BF16)
        max_ref[i : i + 1, :] = top
    for i in range(heads):
        left = jnp.concatenate([turned_ref[i * HD : (i + 1) * HD, :], ones], axis=0)
        update = mm(left, weights_ref[i])[: acc_ref.shape[1], :]
        if before is not None:
            update = before[0][i] * factors[i] + update
        acc_ref[i] = update


def loads(pairs, sems):
    copies = [pltpu.make_async_copy(x, y, sems.at[k]) for k, (x, y) in enumerate(pairs)]

    def start():
        for copy in copies:
            copy.start()

    def wait():
        for copy in copies:
            copy.wait()

    return start, wait


def finish(acc_ref, out_ref):
    for pair in range(acc_ref.shape[0] // 2):
        parts = []
        for i in (2 * pair, 2 * pair + 1):
            parts.append(acc_ref[i, :HD, :] / acc_ref[i, HD : HD + 1, :])
        out_ref[:, pair * LANES : (pair + 1) * LANES] = (
            jnp.concatenate(parts, axis=0).T.astype(BF16)
        )


def opening_kernel(
    packed, got, other, reach_ref, a0, b0, a2_any, b2_any, a1_any, b1_any, q_ref, wk, wv,
    acc_ref, max_ref, keys_ref, turned_ref, down_ref, up_ref, token_ref,
    a2, b2, a1, b1, weights_ref, sems,
):
    count = reach_ref[0, 0]
    odd = lax.axis_index("seq") % 2 == 1
    start, wait = loads(((a2_any, a2), (b2_any, b2), (a1_any, a1), (b1_any, b1)), sems)
    start()
    token_ref[...] = reach_ref[...]
    if packed:
        unpack(got, other, down_ref, up_ref)
    else:
        down_ref[...] = got[...]
        up_ref[...] = other[...]
    state = (acc_ref, max_ref)
    project(a0, b0, wk, wv, down_ref, up_ref, keys_ref, turned_ref)
    attend(q_ref, keys_ref, turned_ref, None, state, weights_ref)
    wait()

    @pl.when(count >= 2)
    def _():
        project(a2, b2, wk, wv, down_ref, up_ref, keys_ref, turned_ref)

    @pl.when(odd & (count >= 2))
    def _():
        attend(q_ref, keys_ref, turned_ref, state, state, weights_ref)

    @pl.when(odd & (count >= 1))
    def _():
        project(a1, b1, wk, wv, down_ref, up_ref, keys_ref, turned_ref)


def middle_kernel(
    reach_ref, ax_any, bx_any, q_ref, wk, wv, down_ref, up_ref, acc_in, max_in, keys_in, turned_in,
    acc_ref, max_ref, keys_ref, turned_ref, token_ref, a, b, weights_ref, sems,
):
    count = reach_ref[0, 0]
    odd = lax.axis_index("seq") % 2 == 1
    needed = count >= jnp.where(odd, 3, 1)
    start, wait = loads(((ax_any, a), (bx_any, b)), sems)
    pl.when(needed)(start)
    token_ref[...] = reach_ref[...]

    @pl.when(count >= jnp.where(odd, 1, 2))
    def _():
        attend(q_ref, keys_in, turned_in, (acc_in, max_in), (acc_ref, max_ref), weights_ref)

    @pl.when(needed)
    def _():
        wait()
        project(a, b, wk, wv, down_ref, up_ref, keys_ref, turned_ref)


def closing_kernel(
    reach_ref, a3_any, b3_any, q_ref, wk, wv, down_ref, up_ref, acc_in, max_in, keys_in, turned_in,
    out_ref, acc_ref, max_ref, keys_ref, turned_ref, a, b, weights_ref, sems,
):
    count = reach_ref[0, 0]
    odd = lax.axis_index("seq") % 2 == 1
    pending = count >= jnp.where(odd, 3, 1)
    needed = (count >= 3) & jnp.logical_not(odd)
    start, wait = loads(((a3_any, a), (b3_any, b)), sems)
    state = (acc_ref, max_ref)
    pl.when(needed)(start)

    @pl.when(pending)
    def _():
        attend(q_ref, keys_in, turned_in, (acc_in, max_in), state, weights_ref)

        @pl.when(needed)
        def _():
            wait()
            project(a, b, wk, wv, down_ref, up_ref, keys_ref, turned_ref)
            attend(q_ref, keys_ref, turned_ref, state, state, weights_ref)

        finish(acc_ref, out_ref)

    @pl.when(jnp.logical_not(pending))
    def _():
        finish(acc_in, out_ref)


def body(
    frames, w_query, w_key, w_value, down_bank, up_bank, bank_row, lang_ids, seg_ids, lookback
):
    count = lax.axis_size("seq")
    rows, width = frames.shape
    columns = w_query.shape[1]
    heads = columns // HD
    model_width = w_query.shape[0]
    rank_two = down_bank.shape[2]
    params = pltpu.CompilerParams(vmem_limit_bytes=VMEM_BYTES)

    def permute(x, route, name):
        with jax.named_scope(name):
            return lax.ppermute(x, "seq", route)

    def swap(x, name):
        with jax.named_scope(name + "_swap"):
            return lax.ppermute(x, "head", [(0, 1), (1, 0)])

    a0 = frames
    b0 = swap(a0, "own")
    q, b0 = pl.pallas_call(
        query_kernel,
        out_shape=(
            jax.ShapeDtypeStruct((columns, rows), BF16),
            jax.ShapeDtypeStruct((rows, width), BF16),
        ),
        in_specs=[HBM()] * 3,
        out_specs=(VMEM(), VMEM()),
        scratch_shapes=[pltpu.VMEM((rows, width), BF16)]
        + [pltpu.VMEM(w_query.shape, BF16), pltpu.SemaphoreType.DMA((3,))],
        compiler_params=params,
        cost_estimate=cost(2),
    )(*(pltpu.with_memory_space_constraint(x, pltpu.HBM) for x in (a0, b0, w_query)))
    near = [(i, i ^ 1) for i in range(count)]
    two = [(i, (i + 2) % count) for i in range(count)]
    pairs = [(i, i) for i in (0, 1, 2, count - 1)]
    pairs += [(i, i + 1 if i % 2 else i - 1) for i in range(3, count - 1)]

    a2 = permute(a0, two, "two")
    b2 = swap(a2, "two")
    a1 = permute(a0, near, "near")
    packed = down_bank.shape[1] % 32 == 0 and up_bank.shape[1] % 16 == 0
    reaching, *sent = rules(
        packed, bank_row, lang_ids, seg_ids, lookback, down_bank, up_bank, count
    )
    if packed:
        got = lax.all_to_all(sent[0], "seq", split_axis=0, concat_axis=0, tiled=True)
        half, reaching = pl.pallas_call(
            lower_kernel,
            out_shape=(
                jax.ShapeDtypeStruct((count, down_bank.shape[1] // 2, LANES), BF16),
                jax.ShapeDtypeStruct((8, LANES), jnp.int32),
            ),
            in_specs=[VMEM()] * 5,
            out_specs=(VMEM(), VMEM()),
            compiler_params=params,
        )(got, q, reaching, w_key, w_value)
        other = swap(half, "down")
    else:
        wanted = jnp.take(bank_row, lang_ids, axis=0)
        got = lax.all_to_all(
            jnp.take(down_bank, wanted, axis=0), "seq", split_axis=0, concat_axis=0, tiled=True
        ).reshape(model_width, rank_two)
        other = lax.all_to_all(
            jnp.take(up_bank, wanted, axis=0), "seq", split_axis=0, concat_axis=0, tiled=True
        ).reshape(rank_two, columns)
    moved = jnp.where(lax.axis_index("head") == 0, a2, a1)
    ways = [(2 * i, 2 * j) for i, j in near] + [(2 * i + 1, 2 * j + 1) for i, j in two]
    with jax.named_scope("split"):
        ax = lax.ppermute(moved, ("seq", "head"), ways)
    a3 = permute(a2, pairs, "rest")
    ax, reaching = lax.optimization_barrier((ax, reaching))
    b1, bx = swap(a1, "near"), swap(ax, "cross")

    state = (
        jax.ShapeDtypeStruct((heads, HD + 8, rows), F32),
        jax.ShapeDtypeStruct((heads, rows), F32),
    )
    weights = pltpu.VMEM((heads, rows, rows), BF16)
    half_frames = pltpu.VMEM((rows, width), BF16)
    projected = (
        jax.ShapeDtypeStruct((rows, columns), BF16),
        jax.ShapeDtypeStruct((columns, rows), BF16),
    )
    token = jax.ShapeDtypeStruct((8, LANES), jnp.int32)
    acc, top, keys, turned, down, up, reached = pl.pallas_call(
        functools.partial(opening_kernel, packed),
        out_shape=state
        + projected
        + (
            jax.ShapeDtypeStruct((model_width, rank_two), BF16),
            jax.ShapeDtypeStruct((rank_two, columns), BF16),
            token,
        ),
        in_specs=[VMEM()] * 5 + [ANY()] * 4 + [VMEM()] * 3,
        out_specs=(VMEM(),) * 7,
        scratch_shapes=[half_frames] * 4 + [weights, pltpu.SemaphoreType.DMA((4,))],
        compiler_params=params,
        cost_estimate=cost(0.1),
    )(got, other, reaching, a0, b0, a2, b2, a1, b1, q, w_key, w_value)
    a3, reached = lax.optimization_barrier((a3, reached))
    acc, top, keys, turned, reached = pl.pallas_call(
        middle_kernel,
        out_shape=state + projected + (token,),
        in_specs=[VMEM()] + [ANY()] * 2 + [VMEM()] * 9,
        out_specs=(VMEM(),) * 5,
        scratch_shapes=[half_frames] * 2 + [weights, pltpu.SemaphoreType.DMA((2,))],
        input_output_aliases={8: 0, 9: 1},
        compiler_params=params,
        cost_estimate=cost(0.1),
    )(reached, ax, bx, q, w_key, w_value, down, up, acc, top, keys, turned)
    b3 = swap(a3, "rest")
    return pl.pallas_call(
        closing_kernel,
        out_shape=jax.ShapeDtypeStruct((rows, columns), BF16),
        in_specs=[VMEM()] + [ANY()] * 2 + [VMEM()] * 9,
        out_specs=VMEM(),
        scratch_shapes=[pltpu.VMEM(s.shape, s.dtype) for s in state + projected]
        + [half_frames] * 2
        + [weights, pltpu.SemaphoreType.DMA((2,))],
        compiler_params=params,
        cost_estimate=cost(0.1),
    )(reached, a3, b3, q, w_key, w_value, down, up, acc, top, keys, turned)


def solution(mesh):
    in_specs = (
        P(("parts", "seq"), "head"),
        P(None, "head"),
        P(None, "head"),
        P(None, "head"),
        P(None, "seq", None),
        P(None, "seq", "head"),
        P(),
        P("parts"),
        P("parts"),
        P("parts"),
    )
    out_specs = P(("parts", "seq"), "head")
    return jax.shard_map(body, mesh=mesh, in_specs=in_specs, out_specs=out_specs, check_vma=False)
```

```python
import functools

import jax
import jax.numpy as jnp
from jax import lax
from jax.experimental import pallas as pl
from jax.experimental.pallas import tpu as pltpu
from jax.sharding import PartitionSpec as P

HD = 64
LANES = 128
LOOK = 3
VMEM_BYTES = 8 * 1024 * 1024
F32 = jnp.float32
BF16 = jnp.bfloat16

VMEM = functools.partial(pl.BlockSpec, memory_space=pltpu.VMEM)
ANY = functools.partial(pl.BlockSpec, memory_space=pl.ANY)
HBM = functools.partial(pl.BlockSpec, memory_space=pltpu.HBM)


def mm(a, b):
    return jnp.dot(a, b, preferred_element_type=F32)


def reach(seg_ref, look_ref, position):
    count = jnp.int32(0)
    for distance in range(1, LOOK + 1):
        earlier = jnp.maximum(position - distance, 0)
        allowed = (
            (position >= distance)
            & (look_ref[position] >= distance)
            & (seg_ref[earlier] == seg_ref[position])
        )
        count = count + allowed.astype(jnp.int32)
    return count


def rules_kernel(
    packed, row_hbm, lang_hbm, seg_hbm, look_hbm, down_hbm, up_hbm, *refs
):
    if packed:
        reach_ref, out_ref, row, lang, seg, look, down, up, sems = refs
        pairs = [(row_hbm, row), (lang_hbm, lang), (seg_hbm, seg), (look_hbm, look)]
        pairs += [(down_hbm, down), (up_hbm, up)]
    else:
        reach_ref, seg, look, sems = refs
        pairs = [(seg_hbm, seg), (look_hbm, look)]
    copies = [pltpu.make_async_copy(a, b, sems.at[k]) for k, (a, b) in enumerate(pairs)]
    for copy in copies:
        copy.start()
    for copy in copies:
        copy.wait()
    count = reach(seg, look, lax.axis_index("seq"))
    reach_ref[...] = jnp.full(reach_ref.shape, count, jnp.int32)
    if packed:
        half = down.shape[1] // 2
        depth = up.shape[1]
        mine = pl.ds(pl.multiple_of(lax.axis_index("head") * half, half), half)
        for j in range(out_ref.shape[0]):
            chosen = row[lang[j]]
            out_ref[j, :half, :] = down[chosen, mine, :]
            for c in range(up.shape[2] // LANES):
                out_ref[j, half + c * depth : half + (c + 1) * depth, :] = up[
                    chosen, :, c * LANES : (c + 1) * LANES
                ]


def cost(microseconds):
    return pl.CostEstimate(flops=int(microseconds * 1e9), bytes_accessed=0, transcendentals=0)


def rules(packed, bank_row, lang_ids, seg_ids, lookback, down_bank, up_bank, count):
    rows = down_bank.shape[1] // 2 + up_bank.shape[1] * (up_bank.shape[2] // LANES)
    out_shape = [jax.ShapeDtypeStruct((8, LANES), jnp.int32)]
    tables = [seg_ids, lookback]
    scratch = []
    if packed:
        out_shape.append(jax.ShapeDtypeStruct((count, rows, LANES), BF16))
        tables = [bank_row, lang_ids] + tables
        scratch = [pltpu.VMEM(down_bank.shape, BF16), pltpu.VMEM(up_bank.shape, BF16)]
    scratch = [pltpu.SMEM(t.shape, jnp.int32) for t in tables] + scratch
    return pl.pallas_call(
        functools.partial(rules_kernel, packed),
        out_shape=out_shape,
        in_specs=[HBM()] * 6,
        out_specs=[VMEM()] * len(out_shape),
        scratch_shapes=scratch + [pltpu.SemaphoreType.DMA((len(scratch),))],
        compiler_params=pltpu.CompilerParams(vmem_limit_bytes=VMEM_BYTES),
        cost_estimate=cost(2),
    )(
        *(
            pltpu.with_memory_space_constraint(x, pltpu.HBM)
            for x in (bank_row, lang_ids, seg_ids, lookback, down_bank, up_bank)
        )
    )


def halves(head, width):
    mine = pl.ds(pl.multiple_of(head * width, width), width)
    other = pl.ds(pl.multiple_of((1 - head) * width, width), width)
    return mine, other


def query_kernel(a_hbm, b_hbm, wq_hbm, q_ref, b, a, wq, sems):
    pairs = ((a_hbm, a), (b_hbm, b), (wq_hbm, wq))
    copies = [pltpu.make_async_copy(x, y, sems.at[k]) for k, (x, y) in enumerate(pairs)]
    for copy in copies:
        copy.start()
    for copy in copies:
        copy.wait()
    mine, other = halves(lax.axis_index("head"), a.shape[1])
    queries = (mm(a[...], wq[mine, :]) + mm(b[...], wq[other, :])).astype(BF16)
    q_ref[...] = (queries * jnp.asarray(HD**-0.5, BF16)).T


def lower_kernel(got, q_ref, reach_ref, wk, wv, half_ref, token_ref):
    token_ref[...] = reach_ref[...]
    half_ref[...] = got[:, : half_ref.shape[1], :]


def unpack(got, other, down_ref, up_ref):
    head = lax.axis_index("head")
    half = other.shape[1]
    depth = up_ref.shape[0] // got.shape[0]
    for j in range(got.shape[0]):
        for part, source in ((head, got), (1 - head, other)):
            place = pl.ds(pl.multiple_of(j * 2 * half + part * half, half), half)
            down_ref[place, :] = source[j, :half, :]
    for c in range(up_ref.shape[1] // LANES):
        piece = got[:, half + c * depth : half + (c + 1) * depth, :]
        up_ref[:, c * LANES : (c + 1) * LANES] = piece.reshape(up_ref.shape[0], LANES)


def project(a, b, wk, wv, down_ref, up_ref, keys_ref, turned_ref, wait=lambda: None):
    mine, other = halves(lax.axis_index("head"), a.shape[1])
    first = a[...]
    keys, values = mm(first, wk[mine, :]), mm(first, wv[mine, :])
    lowrank = mm(first, down_ref[mine, :])
    wait()
    second = b[...]
    lowrank = lowrank + mm(second, down_ref[other, :])
    lowrank = lowrank.astype(BF16)
    lane = lax.broadcasted_iota(jnp.int32, lowrank.shape, 1)
    split = lowrank.shape[1] // 2
    zero = jnp.zeros_like(lowrank)
    low_key = jnp.where(lane < split, lowrank, zero)
    low_value = jnp.where(lane < split, zero, lowrank)
    up = up_ref[...]
    keys = keys + mm(second, wk[other, :]) + mm(low_key, up)
    values = values + mm(second, wv[other, :]) + mm(low_value, up)
    keys_ref[...] = keys.astype(BF16)
    turned_ref[...] = values.astype(BF16).T


def attend(q_ref, keys_ref, turned_ref, before, after, weights_ref):
    keys = keys_ref[...]
    ones = jnp.ones((16, turned_ref.shape[1]), BF16)
    acc_ref, max_ref = after
    heads = acc_ref.shape[0]
    factors = []
    for i in range(heads):
        q = q_ref[i * HD : (i + 1) * HD, :]
        zero = jnp.zeros_like(q)
        q = jnp.concatenate([q, zero] if i % 2 == 0 else [zero, q], axis=0)
        parts = []
        for first in range(0, q.shape[1], LANES):
            cols = slice(first, first + LANES)
            scores = mm(keys[:, i // 2 * LANES : (i // 2 + 1) * LANES], q[:, cols])
            top = jnp.max(scores, axis=0, keepdims=True)
            if before is not None:
                old = before[1][i : i + 1, cols]
                top = jnp.maximum(top, old)
                parts.append(jnp.exp(old - top))
            weights_ref[i, :, cols] = jnp.exp(scores - top).astype(BF16)
            max_ref[i : i + 1, cols] = top
        if before is not None:
            factors.append(jnp.concatenate(parts, axis=1))
    for i in range(heads):
        left = jnp.concatenate([turned_ref[i * HD : (i + 1) * HD, :], ones], axis=0)
        update = mm(left, weights_ref[i])[: acc_ref.shape[1], :]
        if before is not None:
            update = before[0][i] * factors[i] + update
        acc_ref[i] = update


def loads(pairs, sems):
    copies = [pltpu.make_async_copy(x, y, sems.at[k]) for k, (x, y) in enumerate(pairs)]

    def start():
        for copy in copies:
            copy.start()

    def wait():
        for copy in copies:
            copy.wait()

    return start, wait


def finish(acc_ref, out_ref):
    for pair in range(acc_ref.shape[0] // 2):
        parts = []
        for i in (2 * pair, 2 * pair + 1):
            parts.append(acc_ref[i, :HD, :] / acc_ref[i, HD : HD + 1, :])
        out_ref[:, pair * LANES : (pair + 1) * LANES] = (
            jnp.concatenate(parts, axis=0).T.astype(BF16)
        )


def opening_kernel(
    packed, got, other, reach_ref, a0, b0, a2_any, b2_any, a1_any, b1_any, ax_any, q_ref, wk, wv,
    acc_ref, max_ref, down_ref, up_ref, ax_ref, token_ref,
    a2, b2, a1, b1, keys_ref, turned_ref, weights_ref, sems, sems_x,
):
    count = reach_ref[0, 0]
    odd = lax.axis_index("seq") % 2 == 1
    start, wait = loads(((a2_any, a2), (b2_any, b2), (a1_any, a1), (b1_any, b1)), sems)
    start_x, wait_x = loads(((ax_any, ax_ref),), sems_x)
    start()
    start_x()
    token_ref[...] = reach_ref[...]
    if packed:
        unpack(got, other, down_ref, up_ref)
    else:
        down_ref[...] = got[...]
        up_ref[...] = other[...]
    state = (acc_ref, max_ref)
    project(a0, b0, wk, wv, down_ref, up_ref, keys_ref, turned_ref)
    attend(q_ref, keys_ref, turned_ref, None, state, weights_ref)
    wait()

    @pl.when(count >= 2)
    def _():
        project(a2, b2, wk, wv, down_ref, up_ref, keys_ref, turned_ref)

        attend(q_ref, keys_ref, turned_ref, state, state, weights_ref)

    @pl.when(odd & (count >= 1))
    def _():
        project(a1, b1, wk, wv, down_ref, up_ref, keys_ref, turned_ref)
        attend(q_ref, keys_ref, turned_ref, state, state, weights_ref)

    wait_x()


def middle_kernel(
    reach_ref, ax, bx_any, wk, wv, down_ref, up_ref, keys_ref, turned_ref, token_ref, b, sems
):
    odd = lax.axis_index("seq") % 2 == 1
    token_ref[...] = reach_ref[...]

    @pl.when(reach_ref[0, 0] >= jnp.where(odd, 3, 1))
    def _():
        start, wait = loads(((bx_any, b),), sems)
        start()
        project(ax, b, wk, wv, down_ref, up_ref, keys_ref, turned_ref, wait)


def closing_kernel(
    reach_ref, a3_any, b3_any, q_ref, wk, wv, down_ref, up_ref, acc_in, max_in, keys_in, turned_in,
    out_ref, acc_ref, max_ref, keys_ref, turned_ref, a, b, weights_ref, sems,
):
    count = reach_ref[0, 0]
    odd = lax.axis_index("seq") % 2 == 1
    pending = count >= jnp.where(odd, 3, 1)
    needed = (count >= 3) & jnp.logical_not(odd)
    start, wait = loads(((a3_any, a), (b3_any, b)), sems)
    state = (acc_ref, max_ref)
    pl.when(needed)(start)

    @pl.when(pending)
    def _():
        attend(q_ref, keys_in, turned_in, (acc_in, max_in), state, weights_ref)

        @pl.when(needed)
        def _():
            wait()
            project(a, b, wk, wv, down_ref, up_ref, keys_ref, turned_ref)
            attend(q_ref, keys_ref, turned_ref, state, state, weights_ref)

        finish(acc_ref, out_ref)

    @pl.when(jnp.logical_not(pending))
    def _():
        finish(acc_in, out_ref)


def body(
    frames, w_query, w_key, w_value, down_bank, up_bank, bank_row, lang_ids, seg_ids, lookback
):
    count = lax.axis_size("seq")
    rows, width = frames.shape
    columns = w_query.shape[1]
    heads = columns // HD
    model_width = w_query.shape[0]
    rank_two = down_bank.shape[2]
    params = pltpu.CompilerParams(vmem_limit_bytes=VMEM_BYTES)

    def permute(x, route, name):
        with jax.named_scope(name):
            return lax.ppermute(x, "seq", route)

    def swap(x, name):
        with jax.named_scope(name + "_swap"):
            return lax.ppermute(x, "head", [(0, 1), (1, 0)])

    a0 = frames
    b0 = swap(a0, "own")
    q, b0 = pl.pallas_call(
        query_kernel,
        out_shape=(
            jax.ShapeDtypeStruct((columns, rows), BF16),
            jax.ShapeDtypeStruct((rows, width), BF16),
        ),
        in_specs=[HBM()] * 3,
        out_specs=(VMEM(), VMEM()),
        scratch_shapes=[pltpu.VMEM((rows, width), BF16)]
        + [pltpu.VMEM(w_query.shape, BF16), pltpu.SemaphoreType.DMA((3,))],
        compiler_params=params,
        cost_estimate=cost(2),
    )(*(pltpu.with_memory_space_constraint(x, pltpu.HBM) for x in (a0, b0, w_query)))
    near = [(i, i ^ 1) for i in range(count)]
    two = [(i, (i + 2) % count) for i in range(count)]
    pairs = [(i, i) for i in (0, 1, 2, count - 1)]
    pairs += [(i, i + 1 if i % 2 else i - 1) for i in range(3, count - 1)]

    a2 = permute(a0, two, "two")
    b2 = swap(a2, "two")
    a1 = permute(a0, near, "near")
    packed = down_bank.shape[1] % 32 == 0 and up_bank.shape[1] % 16 == 0
    reaching, *sent = rules(
        packed, bank_row, lang_ids, seg_ids, lookback, down_bank, up_bank, count
    )
    if packed:
        got = lax.all_to_all(sent[0], "seq", split_axis=0, concat_axis=0, tiled=True)
        half, reaching = pl.pallas_call(
            lower_kernel,
            out_shape=(
                jax.ShapeDtypeStruct((count, down_bank.shape[1] // 2, LANES), BF16),
                jax.ShapeDtypeStruct((8, LANES), jnp.int32),
            ),
            in_specs=[VMEM()] * 5,
            out_specs=(VMEM(), VMEM()),
            compiler_params=params,
        )(got, q, reaching, w_key, w_value)
        other = swap(half, "down")
    else:
        wanted = jnp.take(bank_row, lang_ids, axis=0)
        got = lax.all_to_all(
            jnp.take(down_bank, wanted, axis=0), "seq", split_axis=0, concat_axis=0, tiled=True
        ).reshape(model_width, rank_two)
        other = lax.all_to_all(
            jnp.take(up_bank, wanted, axis=0), "seq", split_axis=0, concat_axis=0, tiled=True
        ).reshape(rank_two, columns)
    moved = jnp.where(lax.axis_index("head") == 0, a2, a1)
    ways = [(2 * i, 2 * j) for i, j in near] + [(2 * i + 1, 2 * j + 1) for i, j in two]
    with jax.named_scope("split"):
        ax = lax.ppermute(moved, ("seq", "head"), ways)
    a3 = permute(a2, pairs, "rest")
    ax, reaching = lax.optimization_barrier((ax, reaching))
    b1, bx = swap(a1, "near"), swap(ax, "cross")

    state = (
        jax.ShapeDtypeStruct((heads, HD + 8, rows), F32),
        jax.ShapeDtypeStruct((heads, rows), F32),
    )
    weights = pltpu.VMEM((heads, rows, rows), BF16)
    half_frames = pltpu.VMEM((rows, width), BF16)
    projected = (
        jax.ShapeDtypeStruct((rows, columns), BF16),
        jax.ShapeDtypeStruct((columns, rows), BF16),
    )
    token = jax.ShapeDtypeStruct((8, LANES), jnp.int32)
    acc, top, down, up, ax, reached = pl.pallas_call(
        functools.partial(opening_kernel, packed),
        out_shape=state
        + (
            jax.ShapeDtypeStruct((model_width, rank_two), BF16),
            jax.ShapeDtypeStruct((rank_two, columns), BF16),
            jax.ShapeDtypeStruct((rows, width), BF16),
            token,
        ),
        in_specs=[VMEM()] * 5 + [ANY()] * 5 + [VMEM()] * 3,
        out_specs=(VMEM(),) * 6,
        scratch_shapes=[half_frames] * 4
        + [pltpu.VMEM(s.shape, s.dtype) for s in projected]
        + [weights, pltpu.SemaphoreType.DMA((4,)), pltpu.SemaphoreType.DMA((1,))],
        compiler_params=params,
        cost_estimate=cost(0.1),
    )(got, other, reaching, a0, b0, a2, b2, a1, b1, ax, q, w_key, w_value)
    a3, reached = lax.optimization_barrier((a3, reached))
    keys, turned, reached = pl.pallas_call(
        middle_kernel,
        out_shape=projected + (token,),
        in_specs=[VMEM()] * 2 + [ANY()] + [VMEM()] * 4,
        out_specs=(VMEM(),) * 3,
        scratch_shapes=[half_frames, pltpu.SemaphoreType.DMA((1,))],
        compiler_params=params,
        cost_estimate=cost(0.1),
    )(reached, ax, bx, w_key, w_value, down, up)
    b3 = swap(a3, "rest")
    return pl.pallas_call(
        closing_kernel,
        out_shape=jax.ShapeDtypeStruct((rows, columns), BF16),
        in_specs=[VMEM()] + [ANY()] * 2 + [VMEM()] * 9,
        out_specs=VMEM(),
        scratch_shapes=[pltpu.VMEM(s.shape, s.dtype) for s in state + projected]
        + [half_frames] * 2
        + [weights, pltpu.SemaphoreType.DMA((2,))],
        compiler_params=params,
        cost_estimate=cost(0.1),
    )(reached, a3, b3, q, w_key, w_value, down, up, acc, top, keys, turned)


def solution(mesh):
    in_specs = (
        P(("parts", "seq"), "head"),
        P(None, "head"),
        P(None, "head"),
        P(None, "head"),
        P(None, "seq", None),
        P(None, "seq", "head"),
        P(),
        P("parts"),
        P("parts"),
        P("parts"),
    )
    out_specs = P(("parts", "seq"), "head")
    return jax.shard_map(body, mesh=mesh, in_specs=in_specs, out_specs=out_specs, check_vma=False)
```

```python
import functools

import jax
import jax.numpy as jnp
from jax import lax
from jax.experimental import pallas as pl
from jax.experimental.pallas import tpu as pltpu
from jax.sharding import PartitionSpec as P

HD = 64
LANES = 128
LOOK = 3
VMEM_BYTES = 8 * 1024 * 1024
F32 = jnp.float32
BF16 = jnp.bfloat16

VMEM = functools.partial(pl.BlockSpec, memory_space=pltpu.VMEM)
ANY = functools.partial(pl.BlockSpec, memory_space=pl.ANY)
HBM = functools.partial(pl.BlockSpec, memory_space=pltpu.HBM)


def mm(a, b):
    return jnp.dot(a, b, preferred_element_type=F32)


def reach(seg_ref, look_ref, position):
    count = jnp.int32(0)
    for distance in range(1, LOOK + 1):
        earlier = jnp.maximum(position - distance, 0)
        allowed = (
            (position >= distance)
            & (look_ref[position] >= distance)
            & (seg_ref[earlier] == seg_ref[position])
        )
        count = count + allowed.astype(jnp.int32)
    return count


def rules_kernel(
    packed, row_hbm, lang_hbm, seg_hbm, look_hbm, down_hbm, up_hbm, *refs
):
    if packed:
        reach_ref, sent_ref, row, lang, seg, look, down, up, out_ref, sems, out_sems = refs
        half = down.shape[1]
        depth = up.shape[1]
        mine = pl.ds(pl.multiple_of(lax.axis_index("head") * half, half), half)
        pairs = [(row_hbm, row), (lang_hbm, lang), (seg_hbm, seg), (look_hbm, look)]
        pairs += [(down_hbm.at[:, mine, :], down), (up_hbm, up)]
    else:
        reach_ref, seg, look, sems = refs
        pairs = [(seg_hbm, seg), (look_hbm, look)]
    copies = [pltpu.make_async_copy(a, b, sems.at[k]) for k, (a, b) in enumerate(pairs)]
    for copy in copies:
        copy.start()
    for copy in copies:
        copy.wait()
    sends = []
    if packed:
        for j in range(out_ref.shape[0]):
            chosen = row[lang[j]]
            out_ref[j, :half, :] = down[chosen]
            for c in range(up.shape[2] // LANES):
                out_ref[j, half + c * depth : half + (c + 1) * depth, :] = up[
                    chosen, :, c * LANES : (c + 1) * LANES
                ]
            sends.append(pltpu.make_async_copy(out_ref.at[j], sent_ref.at[j], out_sems.at[j]))
            sends[-1].start()
    count = reach(seg, look, lax.axis_index("seq"))
    reach_ref[...] = jnp.full(reach_ref.shape, count, jnp.int32)
    for send in sends:
        send.wait()


def cost(microseconds):
    return pl.CostEstimate(flops=int(microseconds * 1e9), bytes_accessed=0, transcendentals=0)


def rules(packed, bank_row, lang_ids, seg_ids, lookback, down_bank, up_bank, count):
    rows = down_bank.shape[1] // 2 + up_bank.shape[1] * (up_bank.shape[2] // LANES)
    out_shape = [jax.ShapeDtypeStruct((8, LANES), jnp.int32)]
    tables = [seg_ids, lookback]
    scratch = []
    if packed:
        out_shape.append(jax.ShapeDtypeStruct((count, rows, LANES), BF16))
        tables = [bank_row, lang_ids] + tables
        depth, width = down_bank.shape[1:]
        scratch = [pltpu.VMEM((down_bank.shape[0], depth // 2, width), BF16)]
        scratch.append(pltpu.VMEM(up_bank.shape, BF16))
    scratch = [pltpu.SMEM(t.shape, jnp.int32) for t in tables] + scratch
    sems = [pltpu.SemaphoreType.DMA((len(scratch),))]
    if packed:
        scratch.append(pltpu.VMEM((count, rows, LANES), BF16))
        sems.append(pltpu.SemaphoreType.DMA((count,)))
    return pl.pallas_call(
        functools.partial(rules_kernel, packed),
        out_shape=out_shape,
        in_specs=[HBM()] * 6,
        out_specs=[VMEM()] + [HBM()] * (len(out_shape) - 1),
        scratch_shapes=scratch + sems,
        compiler_params=pltpu.CompilerParams(vmem_limit_bytes=VMEM_BYTES),
        cost_estimate=cost(2),
    )(
        *(
            pltpu.with_memory_space_constraint(x, pltpu.HBM)
            for x in (bank_row, lang_ids, seg_ids, lookback, down_bank, up_bank)
        )
    )


def halves(head, width):
    mine = pl.ds(pl.multiple_of(head * width, width), width)
    other = pl.ds(pl.multiple_of((1 - head) * width, width), width)
    return mine, other


def query_kernel(a_hbm, b_hbm, wq_hbm, q_ref, b, a, wq, sems):
    pairs = ((a_hbm, a), (b_hbm, b), (wq_hbm, wq))
    copies = [pltpu.make_async_copy(x, y, sems.at[k]) for k, (x, y) in enumerate(pairs)]
    for copy in copies:
        copy.start()
    for copy in copies:
        copy.wait()
    mine, other = halves(lax.axis_index("head"), a.shape[1])
    queries = (mm(a[...], wq[mine, :]) + mm(b[...], wq[other, :])).astype(BF16)
    q_ref[...] = (queries * jnp.asarray(HD**-0.5, BF16)).T


def lower_kernel(got, q_ref, reach_ref, wk, wv, half_ref, token_ref):
    token_ref[...] = reach_ref[...]
    half_ref[...] = got[:, : half_ref.shape[1], :]


def unpack(got, other, down_ref, up_ref):
    head = lax.axis_index("head")
    half = other.shape[1]
    depth = up_ref.shape[0] // got.shape[0]
    for j in range(got.shape[0]):
        for part, source in ((head, got), (1 - head, other)):
            place = pl.ds(pl.multiple_of(j * 2 * half + part * half, half), half)
            down_ref[place, :] = source[j, :half, :]
    for c in range(up_ref.shape[1] // LANES):
        piece = got[:, half + c * depth : half + (c + 1) * depth, :]
        up_ref[:, c * LANES : (c + 1) * LANES] = piece.reshape(up_ref.shape[0], LANES)


def project(a, b, wk, wv, down_ref, up_ref, keys_ref, turned_ref, wait=lambda: None):
    mine, other = halves(lax.axis_index("head"), a.shape[1])
    first = a[...]
    keys, values = mm(first, wk[mine, :]), mm(first, wv[mine, :])
    lowrank = mm(first, down_ref[mine, :])
    wait()
    second = b[...]
    lowrank = lowrank + mm(second, down_ref[other, :])
    lowrank = lowrank.astype(BF16)
    lane = lax.broadcasted_iota(jnp.int32, lowrank.shape, 1)
    split = lowrank.shape[1] // 2
    zero = jnp.zeros_like(lowrank)
    low_key = jnp.where(lane < split, lowrank, zero)
    low_value = jnp.where(lane < split, zero, lowrank)
    up = up_ref[...]
    keys = keys + mm(second, wk[other, :]) + mm(low_key, up)
    values = values + mm(second, wv[other, :]) + mm(low_value, up)
    keys_ref[...] = keys.astype(BF16)
    turned_ref[...] = values.astype(BF16).T


def attend(q_ref, keys_ref, turned_ref, before, after, weights_ref):
    keys = keys_ref[...]
    ones = jnp.ones((16, turned_ref.shape[1]), BF16)
    acc_ref, max_ref = after
    heads = acc_ref.shape[0]
    factors = []
    for i in range(heads):
        q = q_ref[i * HD : (i + 1) * HD, :]
        zero = jnp.zeros_like(q)
        q = jnp.concatenate([q, zero] if i % 2 == 0 else [zero, q], axis=0)
        parts = []
        for first in range(0, q.shape[1], LANES):
            cols = slice(first, first + LANES)
            scores = mm(keys[:, i // 2 * LANES : (i // 2 + 1) * LANES], q[:, cols])
            top = jnp.max(scores, axis=0, keepdims=True)
            if before is not None:
                old = before[1][i : i + 1, cols]
                top = jnp.maximum(top, old)
                parts.append(jnp.exp(old - top))
            weights_ref[i, :, cols] = jnp.exp(scores - top).astype(BF16)
            max_ref[i : i + 1, cols] = top
        if before is not None:
            factors.append(jnp.concatenate(parts, axis=1))
    for i in range(heads):
        left = jnp.concatenate([turned_ref[i * HD : (i + 1) * HD, :], ones], axis=0)
        update = mm(left, weights_ref[i])[: acc_ref.shape[1], :]
        if before is not None:
            update = before[0][i] * factors[i] + update
        acc_ref[i] = update


def loads(pairs, sems):
    copies = [pltpu.make_async_copy(x, y, sems.at[k]) for k, (x, y) in enumerate(pairs)]

    def start():
        for copy in copies:
            copy.start()

    def wait():
        for copy in copies:
            copy.wait()

    return start, wait


def finish(acc_ref, out_ref):
    for pair in range(acc_ref.shape[0] // 2):
        parts = []
        for i in (2 * pair, 2 * pair + 1):
            parts.append(acc_ref[i, :HD, :] / acc_ref[i, HD : HD + 1, :])
        out_ref[:, pair * LANES : (pair + 1) * LANES] = (
            jnp.concatenate(parts, axis=0).T.astype(BF16)
        )


def opening_kernel(
    packed, got, other, reach_ref, a0, b0, a2_any, b2_any, a1_any, b1_any, ax_any, q_ref, wk, wv,
    acc_ref, max_ref, down_ref, up_ref, ax_ref, token_ref,
    a2, b2, a1, b1, keys_ref, turned_ref, weights_ref, sems, sems_x,
):
    count = reach_ref[0, 0]
    odd = lax.axis_index("seq") % 2 == 1
    start, wait = loads(((a2_any, a2), (b2_any, b2), (a1_any, a1), (b1_any, b1)), sems)
    start_x, wait_x = loads(((ax_any, ax_ref),), sems_x)
    start()
    start_x()
    token_ref[...] = reach_ref[...]
    if packed:
        unpack(got, other, down_ref, up_ref)
    else:
        down_ref[...] = got[...]
        up_ref[...] = other[...]
    state = (acc_ref, max_ref)
    project(a0, b0, wk, wv, down_ref, up_ref, keys_ref, turned_ref)
    attend(q_ref, keys_ref, turned_ref, None, state, weights_ref)
    wait()

    @pl.when(count >= 2)
    def _():
        project(a2, b2, wk, wv, down_ref, up_ref, keys_ref, turned_ref)

        attend(q_ref, keys_ref, turned_ref, state, state, weights_ref)

    @pl.when(odd & (count >= 1))
    def _():
        project(a1, b1, wk, wv, down_ref, up_ref, keys_ref, turned_ref)
        attend(q_ref, keys_ref, turned_ref, state, state, weights_ref)

    wait_x()


def middle_kernel(
    reach_ref, ax, bx_any, wk, wv, down_ref, up_ref, keys_ref, turned_ref, token_ref, b, sems
):
    odd = lax.axis_index("seq") % 2 == 1
    token_ref[...] = reach_ref[...]

    @pl.when(reach_ref[0, 0] >= jnp.where(odd, 3, 1))
    def _():
        start, wait = loads(((bx_any, b),), sems)
        start()
        project(ax, b, wk, wv, down_ref, up_ref, keys_ref, turned_ref, wait)


def closing_kernel(
    reach_ref, a3_any, b3_any, q_ref, wk, wv, down_ref, up_ref, acc_in, max_in, keys_in, turned_in,
    out_ref, acc_ref, max_ref, keys_ref, turned_ref, a, b, weights_ref, sems,
):
    count = reach_ref[0, 0]
    odd = lax.axis_index("seq") % 2 == 1
    pending = count >= jnp.where(odd, 3, 1)
    needed = (count >= 3) & jnp.logical_not(odd)
    start, wait = loads(((a3_any, a), (b3_any, b)), sems)
    state = (acc_ref, max_ref)
    pl.when(needed)(start)

    @pl.when(pending)
    def _():
        attend(q_ref, keys_in, turned_in, (acc_in, max_in), state, weights_ref)

        @pl.when(needed)
        def _():
            wait()
            project(a, b, wk, wv, down_ref, up_ref, keys_ref, turned_ref)
            attend(q_ref, keys_ref, turned_ref, state, state, weights_ref)

        finish(acc_ref, out_ref)

    @pl.when(jnp.logical_not(pending))
    def _():
        finish(acc_in, out_ref)


def body(
    frames, w_query, w_key, w_value, down_bank, up_bank, bank_row, lang_ids, seg_ids, lookback
):
    count = lax.axis_size("seq")
    rows, width = frames.shape
    columns = w_query.shape[1]
    heads = columns // HD
    model_width = w_query.shape[0]
    rank_two = down_bank.shape[2]
    params = pltpu.CompilerParams(vmem_limit_bytes=VMEM_BYTES)

    def permute(x, route, name):
        with jax.named_scope(name):
            return lax.ppermute(x, "seq", route)

    def swap(x, name):
        with jax.named_scope(name + "_swap"):
            return lax.ppermute(x, "head", [(0, 1), (1, 0)])

    a0 = frames
    b0 = swap(a0, "own")
    q, b0 = pl.pallas_call(
        query_kernel,
        out_shape=(
            jax.ShapeDtypeStruct((columns, rows), BF16),
            jax.ShapeDtypeStruct((rows, width), BF16),
        ),
        in_specs=[HBM()] * 3,
        out_specs=(VMEM(), VMEM()),
        scratch_shapes=[pltpu.VMEM((rows, width), BF16)]
        + [pltpu.VMEM(w_query.shape, BF16), pltpu.SemaphoreType.DMA((3,))],
        compiler_params=params,
        cost_estimate=cost(2),
    )(*(pltpu.with_memory_space_constraint(x, pltpu.HBM) for x in (a0, b0, w_query)))
    near = [(i, i ^ 1) for i in range(count)]
    two = [(i, (i + 2) % count) for i in range(count)]
    pairs = [(i, i) for i in (0, 1, 2, count - 1)]
    pairs += [(i, i + 1 if i % 2 else i - 1) for i in range(3, count - 1)]

    a2 = permute(a0, two, "two")
    b2 = swap(a2, "two")
    a1 = permute(a0, near, "near")
    packed = down_bank.shape[1] % 32 == 0 and up_bank.shape[1] % 16 == 0
    reaching, *sent = rules(
        packed, bank_row, lang_ids, seg_ids, lookback, down_bank, up_bank, count
    )
    if packed:
        got = lax.all_to_all(sent[0], "seq", split_axis=0, concat_axis=0, tiled=True)
        half, reaching = pl.pallas_call(
            lower_kernel,
            out_shape=(
                jax.ShapeDtypeStruct((count, down_bank.shape[1] // 2, LANES), BF16),
                jax.ShapeDtypeStruct((8, LANES), jnp.int32),
            ),
            in_specs=[VMEM()] * 5,
            out_specs=(VMEM(), VMEM()),
            compiler_params=params,
        )(got, q, reaching, w_key, w_value)
        other = swap(half, "down")
    else:
        wanted = jnp.take(bank_row, lang_ids, axis=0)
        got = lax.all_to_all(
            jnp.take(down_bank, wanted, axis=0), "seq", split_axis=0, concat_axis=0, tiled=True
        ).reshape(model_width, rank_two)
        other = lax.all_to_all(
            jnp.take(up_bank, wanted, axis=0), "seq", split_axis=0, concat_axis=0, tiled=True
        ).reshape(rank_two, columns)
    moved = jnp.where(lax.axis_index("head") == 0, a2, a1)
    ways = [(2 * i, 2 * j) for i, j in near] + [(2 * i + 1, 2 * j + 1) for i, j in two]
    with jax.named_scope("split"):
        ax = lax.ppermute(moved, ("seq", "head"), ways)
    a3 = permute(a2, pairs, "rest")
    ax, reaching = lax.optimization_barrier((ax, reaching))
    b1, bx = swap(a1, "near"), swap(ax, "cross")

    state = (
        jax.ShapeDtypeStruct((heads, HD + 8, rows), F32),
        jax.ShapeDtypeStruct((heads, rows), F32),
    )
    weights = pltpu.VMEM((heads, rows, rows), BF16)
    half_frames = pltpu.VMEM((rows, width), BF16)
    projected = (
        jax.ShapeDtypeStruct((rows, columns), BF16),
        jax.ShapeDtypeStruct((columns, rows), BF16),
    )
    token = jax.ShapeDtypeStruct((8, LANES), jnp.int32)
    acc, top, down, up, ax, reached = pl.pallas_call(
        functools.partial(opening_kernel, packed),
        out_shape=state
        + (
            jax.ShapeDtypeStruct((model_width, rank_two), BF16),
            jax.ShapeDtypeStruct((rank_two, columns), BF16),
            jax.ShapeDtypeStruct((rows, width), BF16),
            token,
        ),
        in_specs=[VMEM()] * 5 + [ANY()] * 5 + [VMEM()] * 3,
        out_specs=(VMEM(),) * 6,
        scratch_shapes=[half_frames] * 4
        + [pltpu.VMEM(s.shape, s.dtype) for s in projected]
        + [weights, pltpu.SemaphoreType.DMA((4,)), pltpu.SemaphoreType.DMA((1,))],
        compiler_params=params,
        cost_estimate=cost(0.1),
    )(got, other, reaching, a0, b0, a2, b2, a1, b1, ax, q, w_key, w_value)
    a3, reached = lax.optimization_barrier((a3, reached))
    keys, turned, reached = pl.pallas_call(
        middle_kernel,
        out_shape=projected + (token,),
        in_specs=[VMEM()] * 2 + [ANY()] + [VMEM()] * 4,
        out_specs=(VMEM(),) * 3,
        scratch_shapes=[half_frames, pltpu.SemaphoreType.DMA((1,))],
        compiler_params=params,
        cost_estimate=cost(0.1),
    )(reached, ax, bx, w_key, w_value, down, up)
    b3 = swap(a3, "rest")
    return pl.pallas_call(
        closing_kernel,
        out_shape=jax.ShapeDtypeStruct((rows, columns), BF16),
        in_specs=[VMEM()] + [ANY()] * 2 + [VMEM()] * 9,
        out_specs=VMEM(),
        scratch_shapes=[pltpu.VMEM(s.shape, s.dtype) for s in state + projected]
        + [half_frames] * 2
        + [weights, pltpu.SemaphoreType.DMA((2,))],
        compiler_params=params,
        cost_estimate=cost(0.1),
    )(reached, a3, b3, q, w_key, w_value, down, up, acc, top, keys, turned)


def solution(mesh):
    in_specs = (
        P(("parts", "seq"), "head"),
        P(None, "head"),
        P(None, "head"),
        P(None, "head"),
        P(None, "seq", None),
        P(None, "seq", "head"),
        P(),
        P("parts"),
        P("parts"),
        P("parts"),
    )
    out_specs = P(("parts", "seq"), "head")
    return jax.shard_map(body, mesh=mesh, in_specs=in_specs, out_specs=out_specs, check_vma=False)
```

```python
import functools

import jax
import jax.numpy as jnp
from jax import lax
from jax.experimental import pallas as pl
from jax.experimental.pallas import tpu as pltpu
from jax.sharding import PartitionSpec as P

HD = 64
LANES = 128
LOOK = 3
VMEM_BYTES = 8 * 1024 * 1024
F32 = jnp.float32
BF16 = jnp.bfloat16

VMEM = functools.partial(pl.BlockSpec, memory_space=pltpu.VMEM)
ANY = functools.partial(pl.BlockSpec, memory_space=pl.ANY)
HBM = functools.partial(pl.BlockSpec, memory_space=pltpu.HBM)


def mm(a, b):
    return jnp.dot(a, b, preferred_element_type=F32)


def reach(seg_ref, look_ref, position):
    count = jnp.int32(0)
    for distance in range(1, LOOK + 1):
        earlier = jnp.maximum(position - distance, 0)
        allowed = (
            (position >= distance)
            & (look_ref[position] >= distance)
            & (seg_ref[earlier] == seg_ref[position])
        )
        count = count + allowed.astype(jnp.int32)
    return count


def rules_kernel(
    packed, row_hbm, lang_hbm, seg_hbm, look_hbm, down_hbm, up_hbm, *refs
):
    if packed:
        reach_ref, sent_ref, row, lang, seg, look, down, up, out_ref, sems, out_sems = refs
        half = down.shape[1]
        depth = up.shape[1]
        mine = pl.ds(pl.multiple_of(lax.axis_index("head") * half, half), half)
        pairs = [(row_hbm, row), (lang_hbm, lang), (seg_hbm, seg), (look_hbm, look)]
        pairs += [(down_hbm.at[:, mine, :], down), (up_hbm, up)]
    else:
        reach_ref, seg, look, sems = refs
        pairs = [(seg_hbm, seg), (look_hbm, look)]
    copies = [pltpu.make_async_copy(a, b, sems.at[k]) for k, (a, b) in enumerate(pairs)]
    for copy in copies:
        copy.start()
    for copy in copies:
        copy.wait()
    sends = []
    if packed:
        for j in range(out_ref.shape[0]):
            chosen = row[lang[j]]
            out_ref[j, :half, :] = down[chosen]
            for c in range(up.shape[2] // LANES):
                out_ref[j, half + c * depth : half + (c + 1) * depth, :] = up[
                    chosen, :, c * LANES : (c + 1) * LANES
                ]
            sends.append(pltpu.make_async_copy(out_ref.at[j], sent_ref.at[j], out_sems.at[j]))
            sends[-1].start()
    count = reach(seg, look, lax.axis_index("seq"))
    reach_ref[...] = jnp.full(reach_ref.shape, count, jnp.int32)
    for send in sends:
        send.wait()


def cost(microseconds):
    return pl.CostEstimate(flops=int(microseconds * 1e9), bytes_accessed=0, transcendentals=0)


def rules(packed, bank_row, lang_ids, seg_ids, lookback, down_bank, up_bank, count):
    rows = down_bank.shape[1] // 2 + up_bank.shape[1] * (up_bank.shape[2] // LANES)
    out_shape = [jax.ShapeDtypeStruct((8, LANES), jnp.int32)]
    tables = [seg_ids, lookback]
    scratch = []
    if packed:
        out_shape.append(jax.ShapeDtypeStruct((count, rows, LANES), BF16))
        tables = [bank_row, lang_ids] + tables
        depth, width = down_bank.shape[1:]
        scratch = [pltpu.VMEM((down_bank.shape[0], depth // 2, width), BF16)]
        scratch.append(pltpu.VMEM(up_bank.shape, BF16))
    scratch = [pltpu.SMEM(t.shape, jnp.int32) for t in tables] + scratch
    sems = [pltpu.SemaphoreType.DMA((len(scratch),))]
    if packed:
        scratch.append(pltpu.VMEM((count, rows, LANES), BF16))
        sems.append(pltpu.SemaphoreType.DMA((count,)))
    return pl.pallas_call(
        functools.partial(rules_kernel, packed),
        out_shape=out_shape,
        in_specs=[HBM()] * 6,
        out_specs=[VMEM()] + [HBM()] * (len(out_shape) - 1),
        scratch_shapes=scratch + sems,
        compiler_params=pltpu.CompilerParams(vmem_limit_bytes=VMEM_BYTES),
        cost_estimate=cost(2),
    )(
        *(
            pltpu.with_memory_space_constraint(x, pltpu.HBM)
            for x in (bank_row, lang_ids, seg_ids, lookback, down_bank, up_bank)
        )
    )


def halves(head, width):
    mine = pl.ds(pl.multiple_of(head * width, width), width)
    other = pl.ds(pl.multiple_of((1 - head) * width, width), width)
    return mine, other


def query_kernel(a_hbm, b_hbm, wq_hbm, q_ref, b, a, wq, sems):
    mine, other = halves(lax.axis_index("head"), a.shape[1])
    pairs = (
        (a_hbm, a), (wq_hbm.at[mine, :], wq.at[mine, :]),
        (b_hbm, b), (wq_hbm.at[other, :], wq.at[other, :]),
    )
    copies = [pltpu.make_async_copy(x, y, sems.at[k]) for k, (x, y) in enumerate(pairs)]
    for copy in copies:
        copy.start()
    for copy in copies[:2]:
        copy.wait()
    queries = mm(a[...], wq[mine, :])
    for copy in copies[2:]:
        copy.wait()
    queries = (queries + mm(b[...], wq[other, :])).astype(BF16)
    q_ref[...] = (queries * jnp.asarray(HD**-0.5, BF16)).T


def lower_kernel(got, q_ref, reach_ref, wk, wv, half_ref, token_ref):
    token_ref[...] = reach_ref[...]
    half_ref[...] = got[:, : half_ref.shape[1], :]


def unpack(got, other, down_ref, up_ref):
    head = lax.axis_index("head")
    half = other.shape[1]
    depth = up_ref.shape[0] // got.shape[0]
    for j in range(got.shape[0]):
        for part, source in ((head, got), (1 - head, other)):
            place = pl.ds(pl.multiple_of(j * 2 * half + part * half, half), half)
            down_ref[place, :] = source[j, :half, :]
    for c in range(up_ref.shape[1] // LANES):
        piece = got[:, half + c * depth : half + (c + 1) * depth, :]
        up_ref[:, c * LANES : (c + 1) * LANES] = piece.reshape(up_ref.shape[0], LANES)


def project(a, b, wk, wv, down_ref, up_ref, keys_ref, turned_ref, wait=lambda: None):
    mine, other = halves(lax.axis_index("head"), a.shape[1])
    first = a[...]
    keys, values = mm(first, wk[mine, :]), mm(first, wv[mine, :])
    lowrank = mm(first, down_ref[mine, :])
    wait()
    second = b[...]
    lowrank = lowrank + mm(second, down_ref[other, :])
    lowrank = lowrank.astype(BF16)
    lane = lax.broadcasted_iota(jnp.int32, lowrank.shape, 1)
    split = lowrank.shape[1] // 2
    zero = jnp.zeros_like(lowrank)
    low_key = jnp.where(lane < split, lowrank, zero)
    low_value = jnp.where(lane < split, zero, lowrank)
    up = up_ref[...]
    keys = keys + mm(second, wk[other, :]) + mm(low_key, up)
    values = values + mm(second, wv[other, :]) + mm(low_value, up)
    keys_ref[...] = keys.astype(BF16)
    turned_ref[...] = values.astype(BF16).T


def attend(q_ref, keys_ref, turned_ref, before, after, weights_ref):
    keys = keys_ref[...]
    ones = jnp.ones((16, turned_ref.shape[1]), BF16)
    acc_ref, max_ref = after
    heads = acc_ref.shape[0]
    factors = []
    for i in range(heads):
        q = q_ref[i * HD : (i + 1) * HD, :]
        zero = jnp.zeros_like(q)
        q = jnp.concatenate([q, zero] if i % 2 == 0 else [zero, q], axis=0)
        parts = []
        for first in range(0, q.shape[1], LANES):
            cols = slice(first, first + LANES)
            scores = mm(keys[:, i // 2 * LANES : (i // 2 + 1) * LANES], q[:, cols])
            top = jnp.max(scores, axis=0, keepdims=True)
            if before is not None:
                old = before[1][i : i + 1, cols]
                top = jnp.maximum(top, old)
                parts.append(jnp.exp(old - top))
            weights_ref[i, :, cols] = jnp.exp(scores - top).astype(BF16)
            max_ref[i : i + 1, cols] = top
        if before is not None:
            factors.append(jnp.concatenate(parts, axis=1))
    for i in range(heads):
        left = jnp.concatenate([turned_ref[i * HD : (i + 1) * HD, :], ones], axis=0)
        update = mm(left, weights_ref[i])[: acc_ref.shape[1], :]
        if before is not None:
            update = before[0][i] * factors[i] + update
        acc_ref[i] = update


def loads(pairs, sems):
    copies = [pltpu.make_async_copy(x, y, sems.at[k]) for k, (x, y) in enumerate(pairs)]

    def start():
        for copy in copies:
            copy.start()

    def wait():
        for copy in copies:
            copy.wait()

    return start, wait


def finish(acc_ref, out_ref):
    for pair in range(acc_ref.shape[0] // 2):
        parts = []
        for i in (2 * pair, 2 * pair + 1):
            parts.append(acc_ref[i, :HD, :] / acc_ref[i, HD : HD + 1, :])
        out_ref[:, pair * LANES : (pair + 1) * LANES] = (
            jnp.concatenate(parts, axis=0).T.astype(BF16)
        )


def opening_kernel(
    packed, got, other, reach_ref, a0, b0, a2_any, b2_any, a1_any, b1_any, ax_any, q_ref, wk, wv,
    acc_ref, max_ref, down_ref, up_ref, ax_ref, token_ref,
    a2, b2, a1, b1, keys_ref, turned_ref, weights_ref, sems, sems_x,
):
    count = reach_ref[0, 0]
    odd = lax.axis_index("seq") % 2 == 1
    start, wait = loads(((a2_any, a2), (b2_any, b2), (a1_any, a1), (b1_any, b1)), sems)
    start_x, wait_x = loads(((ax_any, ax_ref),), sems_x)
    start()
    start_x()
    token_ref[...] = reach_ref[...]
    if packed:
        unpack(got, other, down_ref, up_ref)
    else:
        down_ref[...] = got[...]
        up_ref[...] = other[...]
    state = (acc_ref, max_ref)
    project(a0, b0, wk, wv, down_ref, up_ref, keys_ref, turned_ref)
    attend(q_ref, keys_ref, turned_ref, None, state, weights_ref)
    wait()

    @pl.when(count >= 2)
    def _():
        project(a2, b2, wk, wv, down_ref, up_ref, keys_ref, turned_ref)

        attend(q_ref, keys_ref, turned_ref, state, state, weights_ref)

    @pl.when(odd & (count >= 1))
    def _():
        project(a1, b1, wk, wv, down_ref, up_ref, keys_ref, turned_ref)
        attend(q_ref, keys_ref, turned_ref, state, state, weights_ref)

    wait_x()


def middle_kernel(
    reach_ref, ax, bx_any, wk, wv, down_ref, up_ref, keys_ref, turned_ref, token_ref, b, sems
):
    odd = lax.axis_index("seq") % 2 == 1
    token_ref[...] = reach_ref[...]

    @pl.when(reach_ref[0, 0] >= jnp.where(odd, 3, 1))
    def _():
        start, wait = loads(((bx_any, b),), sems)
        start()
        project(ax, b, wk, wv, down_ref, up_ref, keys_ref, turned_ref, wait)


def closing_kernel(
    reach_ref, a3_any, b3_any, q_ref, wk, wv, down_ref, up_ref, acc_in, max_in, keys_in, turned_in,
    out_ref, acc_ref, max_ref, keys_ref, turned_ref, a, b, weights_ref, sems,
):
    count = reach_ref[0, 0]
    odd = lax.axis_index("seq") % 2 == 1
    pending = count >= jnp.where(odd, 3, 1)
    needed = (count >= 3) & jnp.logical_not(odd)
    start, wait = loads(((a3_any, a), (b3_any, b)), sems)
    state = (acc_ref, max_ref)
    pl.when(needed)(start)

    @pl.when(pending)
    def _():
        attend(q_ref, keys_in, turned_in, (acc_in, max_in), state, weights_ref)

        @pl.when(needed)
        def _():
            wait()
            project(a, b, wk, wv, down_ref, up_ref, keys_ref, turned_ref)
            attend(q_ref, keys_ref, turned_ref, state, state, weights_ref)

        finish(acc_ref, out_ref)

    @pl.when(jnp.logical_not(pending))
    def _():
        finish(acc_in, out_ref)


def body(
    frames, w_query, w_key, w_value, down_bank, up_bank, bank_row, lang_ids, seg_ids, lookback
):
    count = lax.axis_size("seq")
    rows, width = frames.shape
    columns = w_query.shape[1]
    heads = columns // HD
    model_width = w_query.shape[0]
    rank_two = down_bank.shape[2]
    params = pltpu.CompilerParams(vmem_limit_bytes=VMEM_BYTES)

    def permute(x, route, name):
        with jax.named_scope(name):
            return lax.ppermute(x, "seq", route)

    def swap(x, name):
        with jax.named_scope(name + "_swap"):
            return lax.ppermute(x, "head", [(0, 1), (1, 0)])

    a0 = frames
    b0 = swap(a0, "own")
    q, b0 = pl.pallas_call(
        query_kernel,
        out_shape=(
            jax.ShapeDtypeStruct((columns, rows), BF16),
            jax.ShapeDtypeStruct((rows, width), BF16),
        ),
        in_specs=[HBM()] * 3,
        out_specs=(VMEM(), VMEM()),
        scratch_shapes=[pltpu.VMEM((rows, width), BF16)]
        + [pltpu.VMEM(w_query.shape, BF16), pltpu.SemaphoreType.DMA((4,))],
        compiler_params=params,
        cost_estimate=cost(2),
    )(*(pltpu.with_memory_space_constraint(x, pltpu.HBM) for x in (a0, b0, w_query)))
    near = [(i, i ^ 1) for i in range(count)]
    two = [(i, (i + 2) % count) for i in range(count)]
    pairs = [(i, i) for i in (0, 1, 2, count - 1)]
    pairs += [(i, i + 1 if i % 2 else i - 1) for i in range(3, count - 1)]

    a2 = permute(a0, two, "two")
    b2 = swap(a2, "two")
    a1 = permute(a0, near, "near")
    packed = down_bank.shape[1] % 32 == 0 and up_bank.shape[1] % 16 == 0
    reaching, *sent = rules(
        packed, bank_row, lang_ids, seg_ids, lookback, down_bank, up_bank, count
    )
    if packed:
        got = lax.all_to_all(sent[0], "seq", split_axis=0, concat_axis=0, tiled=True)
        half, reaching = pl.pallas_call(
            lower_kernel,
            out_shape=(
                jax.ShapeDtypeStruct((count, down_bank.shape[1] // 2, LANES), BF16),
                jax.ShapeDtypeStruct((8, LANES), jnp.int32),
            ),
            in_specs=[VMEM()] * 5,
            out_specs=(VMEM(), VMEM()),
            compiler_params=params,
        )(got, q, reaching, w_key, w_value)
        other = swap(half, "down")
    else:
        wanted = jnp.take(bank_row, lang_ids, axis=0)
        got = lax.all_to_all(
            jnp.take(down_bank, wanted, axis=0), "seq", split_axis=0, concat_axis=0, tiled=True
        ).reshape(model_width, rank_two)
        other = lax.all_to_all(
            jnp.take(up_bank, wanted, axis=0), "seq", split_axis=0, concat_axis=0, tiled=True
        ).reshape(rank_two, columns)
    moved = jnp.where(lax.axis_index("head") == 0, a2, a1)
    ways = [(2 * i, 2 * j) for i, j in near] + [(2 * i + 1, 2 * j + 1) for i, j in two]
    with jax.named_scope("split"):
        ax = lax.ppermute(moved, ("seq", "head"), ways)
    a3 = permute(a2, pairs, "rest")
    ax, reaching = lax.optimization_barrier((ax, reaching))
    b1, bx = swap(a1, "near"), swap(ax, "cross")

    state = (
        jax.ShapeDtypeStruct((heads, HD + 8, rows), F32),
        jax.ShapeDtypeStruct((heads, rows), F32),
    )
    weights = pltpu.VMEM((heads, rows, rows), BF16)
    half_frames = pltpu.VMEM((rows, width), BF16)
    projected = (
        jax.ShapeDtypeStruct((rows, columns), BF16),
        jax.ShapeDtypeStruct((columns, rows), BF16),
    )
    token = jax.ShapeDtypeStruct((8, LANES), jnp.int32)
    acc, top, down, up, ax, reached = pl.pallas_call(
        functools.partial(opening_kernel, packed),
        out_shape=state
        + (
            jax.ShapeDtypeStruct((model_width, rank_two), BF16),
            jax.ShapeDtypeStruct((rank_two, columns), BF16),
            jax.ShapeDtypeStruct((rows, width), BF16),
            token,
        ),
        in_specs=[VMEM()] * 5 + [ANY()] * 5 + [VMEM()] * 3,
        out_specs=(VMEM(),) * 6,
        scratch_shapes=[half_frames] * 4
        + [pltpu.VMEM(s.shape, s.dtype) for s in projected]
        + [weights, pltpu.SemaphoreType.DMA((4,)), pltpu.SemaphoreType.DMA((1,))],
        compiler_params=params,
        cost_estimate=cost(0.1),
    )(got, other, reaching, a0, b0, a2, b2, a1, b1, ax, q, w_key, w_value)
    a3, reached = lax.optimization_barrier((a3, reached))
    keys, turned, reached = pl.pallas_call(
        middle_kernel,
        out_shape=projected + (token,),
        in_specs=[VMEM()] * 2 + [ANY()] + [VMEM()] * 4,
        out_specs=(VMEM(),) * 3,
        scratch_shapes=[half_frames, pltpu.SemaphoreType.DMA((1,))],
        compiler_params=params,
        cost_estimate=cost(0.1),
    )(reached, ax, bx, w_key, w_value, down, up)
    b3 = swap(a3, "rest")
    return pl.pallas_call(
        closing_kernel,
        out_shape=jax.ShapeDtypeStruct((rows, columns), BF16),
        in_specs=[VMEM()] + [ANY()] * 2 + [VMEM()] * 9,
        out_specs=VMEM(),
        scratch_shapes=[pltpu.VMEM(s.shape, s.dtype) for s in state + projected]
        + [half_frames] * 2
        + [weights, pltpu.SemaphoreType.DMA((2,))],
        compiler_params=params,
        cost_estimate=cost(0.1),
    )(reached, a3, b3, q, w_key, w_value, down, up, acc, top, keys, turned)


def solution(mesh):
    in_specs = (
        P(("parts", "seq"), "head"),
        P(None, "head"),
        P(None, "head"),
        P(None, "head"),
        P(None, "seq", None),
        P(None, "seq", "head"),
        P(),
        P("parts"),
        P("parts"),
        P("parts"),
    )
    out_specs = P(("parts", "seq"), "head")
    return jax.shard_map(body, mesh=mesh, in_specs=in_specs, out_specs=out_specs, check_vma=False)
```
